128 devices in a mesh: dp: 16 (over y_hi, z, core), mp: 8 (over x, y_lo).
Axes of the slice: x: 4, y: 4 (y_hi: 2, y_lo: 2; y = y_hi * 2 + y_lo), z: 4, core: 2. Of those that a mesh axis runs over, the one named last changes fastest.
Arguments:
- tokens: bfloat16 [16384, 2048], P('dp'), may hold values from -6 to 6
- doc_lengths: int32 [16, 4], P('dp'), may hold values from 1 to 512, 1024 in all within a row
- gain_one: float32 [2048], P('dp'), may hold values from 0.5 to 1.5
- bias_one: float32 [2048], P('dp'), may hold values from -3 to 3
- w_qkv: float32 [2048, 3, 2048], P('dp', None, 'mp'), may hold values from -0.125 to 0.125
- w_out: float32 [2048, 2048], P('dp', 'mp'), may hold values from -0.75 to 0.75
- gain_two: float32 [2048], P('dp'), may hold values from 0.5 to 1.5
- bias_two: float32 [2048], P('dp'), may hold values from -3 to 3
- w_up: float32 [2048, 8192], P('dp', 'mp'), may hold values from -0.125 to 0.125
- w_down: float32 [2048, 8192], P('dp', 'mp'), may hold values from -0.1875 to 0.1875
- cotangent: bfloat16 [16384, 2048], P('dp'), may hold values from -6 to 6
Outputs:
- output: bfloat16 [16384, 2048], P('dp')
- input_grad: float32 [16384, 2048], P('dp')
- grad_gain_one: float32 [2048], P('dp')
- grad_bias_one: float32 [2048], P('dp')
- grad_qkv: float32 [2048, 3, 2048], P('dp', None, 'mp')
- grad_out: float32 [2048, 2048], P('dp', 'mp')
- grad_gain_two: float32 [2048], P('dp')
- grad_bias_two: float32 [2048], P('dp')
- grad_up: float32 [2048, 8192], P('dp', 'mp')
- grad_down: float32 [2048, 8192], P('dp', 'mp')
The draws below stay inside these ranges and needn't reach their ends.
Inputs may be any that keep to these rules, and one draw needn't show every extreme that they name: `doc_lengths`: the lengths of each row sum to 1024, and in each row the longest document has exactly 512 tokens.
All inputs are finite; a program needn't handle non-finite values.
Results may differ from the reference program's by a relative error of at most 0.013.
The reference program's roundings to bfloat16 on the way count: a program that leaves them out, or rounds other values in their place, can miss the bound.
Values may be sent and summed in bfloat16 or wider, within the bound.
No kernel may reach another device: no remote copies, remote signals or barrier semaphores. Data moves between devices by JAX's collectives and lax.ppermute only.
A program may use at most 192 MiB of HBM per device.

```python
import math
import jax
import jax.numpy as jnp
import numpy as np
from jax import lax

D = 2048
HEADS = 16
HEAD_SIZE = 128
FF = 8192
ROW_TOK = 1024
DOCS = 4
ROWS = 16
TOKENS = 16384


def with_spikes(entries, key, source, target, shards_of, factor):
    def block_of(axis_at):
        return (jnp.arange(entries.shape[axis_at]) // (entries.shape[axis_at] // shards_of)).reshape((-1,) + (1,) * (entries.ndim - 1 - axis_at))

    one_side = jax.random.permutation(key, shards_of)[block_of(target)]
    second = (block_of(target) + shards_of // 2) % shards_of
    return jnp.where((block_of(source) == one_side) | (block_of(source) == second), factor * entries, entries)


def block_scale(own_key, extent, split, low, largest):
    def one(position, blocks):
        heights = jax.random.uniform(jax.random.fold_in(jax.random.fold_in(own_key, 6), position), (blocks,), jnp.float32, low / len(split), largest / len(split))
        return jnp.repeat(jnp.exp(heights), extent[position] // blocks).reshape((-1,) + (1,) * (len(extent) - position - 1))

    level = one(*split[0])
    for cut in split[1:]:
        level = level * one(*cut)
    return level


def profile(number_of, total, reach, lean):
    weights = [(1 << 20) // math.isqrt(grade ** lean) + 1 for grade in range(2, number_of + 1)]
    surplus, counts = total - reach - (number_of - 1), [1] * (number_of - 1)
    while surplus > 0:
        candidates = [i for i in range(number_of - 1) if counts[i] < reach]
        pool, left = sum([weights[i] for i in candidates]), surplus
        for i in candidates:
            extra = min(reach - counts[i], max(1, left * weights[i] // pool), surplus)
            counts[i] = counts[i] + extra
            surplus = surplus - extra
    return np.array([reach] + counts)


def ragged(rng, amount, total, most, lean):
    if amount == 2:
        one = jax.random.randint(rng, (), max(1, total - most), min(most, total - 1) + 1)
        return jnp.stack([one, total - one])
    tallies = jnp.asarray(profile(amount, total, most, lean), jnp.int32)
    twos = (amount - 1) // 2
    donor, taker = tallies[1:1 + 2 * twos:2], tallies[2:2 + 2 * twos:2]
    room = jnp.minimum(donor - 1, most - taker)
    moved = jax.random.randint(jax.random.fold_in(rng, 1), (twos,), 0, 1 << 20) % (room + 1)
    tallies = tallies.at[1:1 + 2 * twos:2].set(donor - moved).at[2:2 + 2 * twos:2].set(taker + moved)
    return tallies[jax.random.permutation(jax.random.fold_in(rng, 2), amount)]


def scatter_about(key, dims, width, limit, pieces=(), kind=jnp.bfloat16):
    level = block_scale(key, dims, pieces, -0.22, 0.18) if pieces else 1.0
    drawn = jax.random.normal(key, dims, jnp.float32) * width * level
    return jnp.minimum(jnp.maximum(drawn, -limit), limit).astype(kind)


def noise_with(own_key, extent, spread, reach, cuts, heavy, held_as=jnp.bfloat16):
    array = spread * jax.random.normal(own_key, extent, jnp.float32)
    if cuts:
        array = array * block_scale(own_key, extent, cuts, -0.22, 0.18)
    return jnp.clip(with_spikes(array, jax.random.fold_in(own_key, 3), *heavy), -reach, reach).astype(held_as)


def setup_inputs(seed: int = 0) -> dict:
    key_list = jax.random.split(jax.random.key(seed), 12)
    tokens = scatter_about(key_list[0], (TOKENS, D), 1.0, 6.0, ((0, 16),))
    doc_lengths = jax.vmap(lambda own: ragged(own, DOCS, ROW_TOK, ROW_TOK // 2, 2))(jax.random.split(key_list[1], ROWS)).reshape((ROWS, DOCS)).astype(jnp.int32)
    gain_one = jnp.clip(1.0 + 0.1 * jax.random.normal(key_list[2], (D,), jnp.float32), 0.5, 1.5)
    bias_one = scatter_about(key_list[3], (D,), 0.5, 3.0, ((0, 16),), jnp.float32)
    w_qkv = scatter_about(key_list[4], (D, 3, D), D ** -0.5, 0.125, ((0, 16), (2, 8)), jnp.float32)
    w_out = scatter_about(key_list[5], (D, D), (D // 32) ** -0.5, 0.75, ((0, 16), (1, 8)), jnp.float32)
    gain_two = jnp.clip(1.0 + 0.1 * jax.random.normal(key_list[6], (D,), jnp.float32), 0.5, 1.5)
    bias_two = scatter_about(key_list[7], (D,), 0.5, 3.0, ((0, 16),), jnp.float32)
    w_up = scatter_about(key_list[8], (D, FF), D ** -0.5, 0.125, ((0, 16), (1, 8)), jnp.float32)
    w_down = noise_with(key_list[9], (D, FF), (FF // 4) ** -0.5, 0.1875, ((0, 16), (1, 8)), (1, 0, 16, 2.0), jnp.float32)
    cotangent = scatter_about(key_list[10], (TOKENS, D), 1.0, 6.0, ((0, 16),))
    return dict(tokens=tokens, doc_lengths=doc_lengths, gain_one=gain_one, bias_one=bias_one, w_qkv=w_qkv, w_out=w_out, gain_two=gain_two, bias_two=bias_two, w_up=w_up, w_down=w_down, cotangent=cotangent)


eps = 1e-05
highest = lax.Precision.HIGHEST

@jax.custom_vjp
def low(v):
    return lax.optimization_barrier(v.astype(jnp.bfloat16)).astype(jnp.float32)

@jax.custom_vjp
def low_back(v):
    return v

def low_keep(v):
    return (low(v), None)

def low_pass(kept, grad):
    return (grad,)

def back_keep(v):
    return (v, None)

def back_low(kept, grad):
    return (low(grad),)
low.defvjp(low_keep, low_pass)
low_back.defvjp(back_keep, back_low)

def layer_norm(values, gain, shift):
    center = values - lax.optimization_barrier(jnp.mean(values, axis=-1, keepdims=True))
    scaled = center * lax.rsqrt(lax.optimization_barrier(jnp.mean(center * center, axis=-1, keepdims=True)) + eps)
    return scaled * gain + shift

def doc_numbers(lengths):
    ends = jnp.cumsum(lengths.astype(jnp.int32))
    places = jnp.arange(ROW_TOK, dtype=jnp.int32)
    return lax.optimization_barrier(jnp.sum((places[:, None] >= ends[None, :]).astype(jnp.int32), axis=1)).astype(jnp.int32)

def attend_row(inputs):
    query, key_row, value_row, docs = inputs
    scores = jnp.einsum('qhe,khe->hqk', query, key_row, precision=highest) / jnp.sqrt(jnp.float32(HEAD_SIZE))
    scores = low_back(scores)
    places = jnp.arange(ROW_TOK, dtype=jnp.int32)
    allowed = (docs[:, None] == docs[None, :]) & (places[None, :] <= places[:, None])
    scores = jnp.where(allowed[None], scores, jnp.float32(-1e+30))
    weights = low(jax.nn.softmax(scores, axis=-1))
    return jnp.einsum('hqk,khe->qhe', weights, value_row, precision=highest)

def forward(inputs, docs, gain_one, bias_one, w_qkv, w_out, gain_two, bias_two, w_up, w_down):
    first = low(layer_norm(inputs, low(gain_one), low(bias_one)))
    mixed = jnp.einsum('td,dcf->tcf', first, low(w_qkv), precision=highest)
    mixed = low_back(low(mixed)).reshape(ROWS, ROW_TOK, 3, HEADS, HEAD_SIZE)
    attended = lax.map(jax.checkpoint(attend_row), (mixed[:, :, 0], mixed[:, :, 1], mixed[:, :, 2], docs))
    attended = low_back(low(attended.reshape(TOKENS, D)))
    branch = low_back(jnp.dot(attended, low(w_out).T, precision=highest))
    middle = inputs + branch
    second = low(layer_norm(middle, low(gain_two), low(bias_two)))
    hidden = low_back(jnp.dot(second, low(w_up), precision=highest))
    active = low(jax.nn.gelu(hidden, approximate=True))
    branch_two = low_back(jnp.dot(active, low(w_down).T, precision=highest))
    return middle + branch_two

def reference(tokens, doc_lengths, gain_one, bias_one, w_qkv, w_out, gain_two, bias_two, w_up, w_down, cotangent):
    docs = jax.vmap(doc_numbers)(doc_lengths)
    inputs = tokens.astype(jnp.float32)

    def wrapped(inputs, gain_one, bias_one, w_qkv, w_out, gain_two, bias_two, w_up, w_down):
        return forward(inputs, docs, gain_one, bias_one, w_qkv, w_out, gain_two, bias_two, w_up, w_down)
    result, pullback = jax.vjp(wrapped, inputs, gain_one, bias_one, w_qkv, w_out, gain_two, bias_two, w_up, w_down)
    grads = pullback(cotangent.astype(jnp.float32))
    return (result.astype(jnp.bfloat16), grads[0], grads[1], grads[2], grads[3], grads[4], grads[5], grads[6], grads[7], grads[8])
```

```python
import jax
import jax.numpy as jnp
from jax import lax
from jax.sharding import Mesh, PartitionSpec as P

HEAD_SIZE = 128
eps = 1e-05
bf16 = jnp.bfloat16
f32 = jnp.float32

NX, NYL, NZ, NYH, NC = 4, 2, 4, 2, 2
MP = ("x", "yl")
DP = ("yh", "z", "c")
CMP = ("c", "x", "yl")


def up(values):
    return values.astype(f32)


def normalize(values):
    center = values - jnp.mean(values, axis=-1, keepdims=True)
    inverse_std = lax.rsqrt(jnp.mean(center * center, axis=-1, keepdims=True) + eps)
    return (center * inverse_std, inverse_std)


def norm_back(grad_norm, normed, inverse_std, gain):
    scaled = grad_norm * gain
    return inverse_std * (
        scaled
        - jnp.mean(scaled, axis=-1, keepdims=True)
        - normed * jnp.mean(scaled * normed, axis=-1, keepdims=True)
    )


def to_xp(x, y):
    return (x + 1, y)


def to_xm(x, y):
    return (x - 1, y)


def to_y(x, y):
    return (x, y + 1)


def send(values, zero, one):
    pairs = []
    for c in range(NC):
        for x in range(NX):
            for y in range(NYL):
                tx, ty = (zero, one)[c](x, y)
                pairs.append(((c * NX + x) * NYL + y, (c * NX + tx % NX) * NYL + ty % NYL))
    return lax.ppermute(values, CMP, pairs)


def halves(values):
    middle = values.shape[0] // 2
    return values[:middle], values[middle:]


def gather_blocks(own):
    core = lax.axis_index("c")

    def pick(zero, one):
        return jnp.where(core == 0, zero, one)

    p1 = send(own, to_xp, to_xp)
    p2 = send(own, to_xm, to_xm)
    q = send(own, to_y, to_y)
    o1 = send(halves(p1)[0], to_xp, to_xp)
    o2 = send(halves(p2)[1], to_xm, to_xm)
    r1 = send(pick(p1, q), to_y, to_xp)
    r2 = send(pick(p2, q), to_y, to_xm)
    s1 = send(pick(o1, halves(r1)[0]), to_y, to_xp)
    s2 = send(pick(o2, halves(r2)[1]), to_y, to_xm)
    return {
        (0, 0): (own,),
        (1, 0): (p2,),
        (2, 0): (o1, o2),
        (3, 0): (p1,),
        (0, 1): (q,),
        (1, 1): (r2,),
        (2, 1): (s1, s2),
        (3, 1): (r1,),
    }


def scatter_sum(blocks):
    core = lax.axis_index("c")
    zero = jnp.where(core == 0, 1.0, 0.0).astype(f32)
    one = 1.0 - zero

    def add_half(block, piece, which, factor):
        first, second = halves(up(block))
        if which == 0:
            first = first + factor * up(piece)
        else:
            second = second + factor * up(piece)
        return jnp.concatenate([first, second], 0)

    h1, h2 = halves(blocks[2, 1])
    s1 = send(h1, to_y, to_xp)
    s2 = send(h2, to_y, to_xm)
    p = send(add_half(blocks[1, 1], s1, 0, one).astype(bf16), to_y, to_xp)
    q = send(add_half(blocks[3, 1], s2, 1, one).astype(bf16), to_y, to_xm)
    g1, g2 = halves(up(blocks[2, 0]))
    r1 = send((g1 + zero * up(s1)).astype(bf16), to_xp, to_xp)
    r2 = send((g2 + zero * up(s2)).astype(bf16), to_xm, to_xm)
    u = send((up(blocks[0, 1]) + one * (up(p) + up(q))).astype(bf16), to_y, to_y)
    t1 = send((add_half(blocks[1, 0], r1, 0, 1.0) + zero * up(p)).astype(bf16), to_xp, to_xp)
    t2 = send((add_half(blocks[3, 0], r2, 1, 1.0) + zero * up(q)).astype(bf16), to_xm, to_xm)
    return up(blocks[0, 0]) + up(t1) + up(t2) + up(u)


REL = [(dx, dy) for dy in range(NYL) for dx in range(NX)]


def to_relative(values):
    x, y = lax.axis_index("x"), lax.axis_index("yl")
    rows = values.shape[0] // (NX * NYL)
    parts = []
    for dx, dy in REL:
        block = ((x + dx) % NX) * NYL + (y + dy) % NYL
        parts.append(lax.dynamic_slice_in_dim(values, block * rows, rows, 0))
    return jnp.concatenate(parts, 0)


def to_row_order(values):
    x, y = lax.axis_index("x"), lax.axis_index("yl")
    rows = values.shape[0] // (NX * NYL)
    parts = []
    for bx in range(NX):
        for by in range(NYL):
            place = ((by - y) % NYL) * NX + (bx - x) % NX
            parts.append(lax.dynamic_slice_in_dim(values, place * rows, rows, 0))
    return jnp.concatenate(parts, 0)


def split_blocks(values):
    rows = values.shape[0] // len(REL)
    return {key: values[i * rows : (i + 1) * rows] for i, key in enumerate(REL)}


def join_blocks(blocks):
    return jnp.concatenate([piece for key in REL for piece in blocks[key]], 0)


def gather_direct(own):
    yh, z, core = lax.axis_index("yh"), lax.axis_index("z"), lax.axis_index("c")
    got = []
    for dy in range(NYH):
        for dz in range(NZ):
            if dy == 0 and dz == 0:
                got.append(own)
                continue
            pairs = [
                (((a + dy) % NYH) * NZ + (b + dz) % NZ, a * NZ + b)
                for a in range(NYH)
                for b in range(NZ)
            ]
            got.append(lax.ppermute(own, ("yh", "z"), pairs))
    mine = jnp.stack(got, 0)
    other = lax.ppermute(mine, "c", [(0, 1), (1, 0)])
    parts = []
    for a in range(NYH):
        for b in range(NZ):
            place = ((a - yh) % NYH) * NZ + (b - z) % NZ
            one = lax.dynamic_index_in_dim(mine, place, 0, keepdims=False)
            two = lax.dynamic_index_in_dim(other, place, 0, keepdims=False)
            parts.append(jnp.where(core == 0, one, two))
            parts.append(jnp.where(core == 0, two, one))
    return jnp.stack(parts, 0)


def scatter_dp(values):
    yh, z, core = lax.axis_index("yh"), lax.axis_index("z"), lax.axis_index("c")
    rows = values.shape[0] // (NYH * NZ * NC)
    parts = values.reshape(NYH, NZ, NC, rows, values.shape[1])

    def of_core(which):
        return lax.dynamic_index_in_dim(parts, which, 2, keepdims=False)

    swapped = lax.ppermute(of_core(1 - core), "c", [(0, 1), (1, 0)])
    both = (up(of_core(core)) + up(swapped)).astype(bf16)

    def of_z(dz):
        return lax.dynamic_index_in_dim(both, (z + dz) % NZ, 1, keepdims=False)

    total = up(of_z(0))
    for dz in (1, 3, 2):
        total = total + up(lax.ppermute(of_z(dz), "z", [(i, (i + dz) % NZ) for i in range(NZ)]))
    total = total.astype(bf16)
    away = lax.dynamic_index_in_dim(total, 1 - yh, 0, keepdims=False)
    home = lax.dynamic_index_in_dim(total, yh, 0, keepdims=False)
    return up(home) + up(lax.ppermute(away, "yh", [(0, 1), (1, 0)]))


def sum_vectors(vectors):
    count, width = vectors.shape
    slices = NYH * NZ * NC
    apart = vectors.reshape(count, slices, width // slices).transpose(1, 0, 2)
    got = lax.all_to_all(apart, DP, split_axis=0, concat_axis=0, tiled=True)
    part = jnp.sum(got, axis=0)
    copies = jnp.broadcast_to(part[None], (NX * NYL,) + part.shape)
    return jnp.sum(lax.all_to_all(copies, MP, split_axis=0, concat_axis=0, tiled=True), axis=0)


def block_scores(query_block, keys, doc_index, begin, block_rows, scale):
    scores = (
        jnp.einsum("qhe,khe->hqk", query_block, keys, preferred_element_type=f32) * scale
    )
    seq_len = keys.shape[0]
    places = jnp.arange(seq_len, dtype=jnp.int32)
    query_places = begin + jnp.arange(block_rows, dtype=jnp.int32)
    query_docs = lax.dynamic_slice_in_dim(doc_index, begin, block_rows, 0)
    allowed = (query_docs[:, None] == doc_index[None, :]) & (
        places[None, :] <= query_places[:, None]
    )
    return jnp.where(allowed[None], scores, f32(-1e30))


def attend(queries, keys, values, doc_index, scale):
    seq_len = queries.shape[0]
    block_rows = min(512, seq_len)
    out, lse = [], []
    for begin in range(0, seq_len, block_rows):
        scores = block_scores(
            queries[begin : begin + block_rows], keys, doc_index, begin, block_rows, scale
        )
        largest = jnp.max(scores, axis=-1, keepdims=True)
        expo = jnp.exp(scores - largest)
        totals = jnp.sum(expo, axis=-1, keepdims=True)
        probs = (expo / totals).astype(bf16)
        lse.append((largest + jnp.log(totals))[..., 0])
        out.append(jnp.einsum("hqk,khe->qhe", probs, values, preferred_element_type=f32))
    return jnp.concatenate(out, axis=0), jnp.concatenate(lse, axis=1)


def attend_back(queries, keys, values, lse, grad_out, doc_index, scale):
    seq_len = queries.shape[0]
    block_rows = min(512, seq_len)
    grad_queries = []
    grad_keys = jnp.zeros(keys.shape, f32)
    grad_values = jnp.zeros(keys.shape, f32)
    for begin in range(0, seq_len, block_rows):
        query_block = queries[begin : begin + block_rows]
        scores = block_scores(query_block, keys, doc_index, begin, block_rows, scale)
        probs = jnp.exp(scores - lse[:, begin : begin + block_rows, None])
        grad_block = grad_out[begin : begin + block_rows]
        grad_probs = jnp.einsum("qhe,khe->hqk", grad_block, values, preferred_element_type=f32)
        inner = jnp.sum(probs * grad_probs, axis=-1, keepdims=True)
        grad_scores = (probs * (grad_probs - inner)).astype(bf16)
        grad_queries.append(
            jnp.einsum("hqk,khe->qhe", grad_scores, keys, preferred_element_type=f32) * scale
        )
        grad_keys = (
            grad_keys
            + jnp.einsum("hqk,qhe->khe", grad_scores, query_block, preferred_element_type=f32)
            * scale
        )
        grad_values = grad_values + jnp.einsum(
            "hqk,qhe->khe", probs.astype(bf16), grad_block, preferred_element_type=f32
        )
    return jnp.concatenate(grad_queries, axis=0), grad_keys, grad_values


def local(
    tokens,
    doc_lengths,
    gain_one,
    bias_one,
    w_qkv,
    w_out,
    gain_two,
    bias_two,
    w_up,
    w_down,
    cotangent,
):
    seq_len, width = tokens.shape
    shard = w_qkv.shape[0]
    local_width = w_qkv.shape[2]
    local_heads = local_width // HEAD_SIZE
    rows = seq_len // (NX * NYL)
    x, y = lax.axis_index("x"), lax.axis_index("yl")
    my_rows = (x * NYL + y) * rows
    scale = 1.0 / jnp.sqrt(f32(HEAD_SIZE))

    small = jnp.stack([gain_one, bias_one, gain_two, bias_two], 0).astype(bf16)
    small = jnp.pad(small.reshape(1, -1), ((0, 15), (0, 0)))
    columns = max(3 * local_width, small.shape[1])
    packed = jnp.concatenate(
        [
            jnp.pad(
                w_qkv.reshape(shard, 3 * local_width).astype(bf16),
                ((0, 0), (0, columns - 3 * local_width)),
            ),
            jnp.pad(small, ((0, 0), (0, columns - small.shape[1]))),
        ],
        0,
    )
    first_full = gather_direct(packed)
    qkv_weight = first_full[:, :shard, : 3 * local_width].reshape(width, 3 * local_width)
    vectors = (
        first_full[:, shard, : 4 * shard].reshape(-1, 4, shard).transpose(1, 0, 2).reshape(4, width)
    )
    gain_a, bias_a, gain_b, bias_b = (up(vectors[i]) for i in range(4))
    up_weight = lax.all_gather(w_up.astype(bf16), DP, axis=0, tiled=True)
    down_weight = lax.all_gather(w_down.astype(bf16), DP, axis=0, tiled=True)
    out_weight = gather_direct(w_out.astype(bf16)).reshape(width, local_width)

    ends = jnp.cumsum(doc_lengths[0])
    positions = jnp.arange(seq_len, dtype=jnp.int32)
    doc_index = jnp.sum((positions[:, None] >= ends[None, :]).astype(jnp.int32), axis=1)

    normed_one, _ = normalize(up(tokens))
    first = (normed_one * gain_a + bias_a).astype(bf16)
    mixed = jnp.dot(first, qkv_weight, preferred_element_type=f32).astype(bf16)
    mixed = mixed.reshape(seq_len, 3, local_heads, HEAD_SIZE)
    queries, keys, values = mixed[:, 0], mixed[:, 1], mixed[:, 2]
    attended, lse = attend(queries, keys, values, doc_index, scale)
    attended = attended.reshape(seq_len, local_width).astype(bf16)
    attended = to_relative(attended)
    terms = jnp.einsum("tf,df->td", attended, out_weight, preferred_element_type=f32).astype(bf16)
    own_tokens = up(lax.dynamic_slice_in_dim(tokens, my_rows, rows, 0))
    own_cot = up(lax.dynamic_slice_in_dim(cotangent, my_rows, rows, 0))
    middle = own_tokens + scatter_sum(split_blocks(terms))

    normed_two, inverse_two = normalize(middle)
    second_own = (normed_two * gain_b + bias_b).astype(bf16)
    second = join_blocks(gather_blocks(second_own))
    cot_rel = to_relative(cotangent)
    grad_active = jnp.dot(cot_rel, down_weight, preferred_element_type=f32)
    hidden = jnp.dot(second, up_weight, preferred_element_type=f32)

    def gelu_tanh(values_in):
        return jax.nn.gelu(values_in, approximate=True)

    active_f, gelu_pull = jax.vjp(gelu_tanh, hidden)
    active = active_f.astype(bf16)
    grad_hidden = gelu_pull(grad_active)[0].astype(bf16)
    second_terms = jnp.einsum(
        "tf,df->td", grad_hidden, up_weight, preferred_element_type=f32
    ).astype(bf16)
    grad_second = scatter_sum(split_blocks(second_terms))
    down_terms = jnp.einsum(
        "tf,df->td", to_row_order(active), down_weight, preferred_element_type=f32
    ).astype(bf16)
    branch_two = lax.psum_scatter(down_terms, MP, scatter_dimension=0, tiled=True)
    output_own = (middle + up(branch_two)).astype(bf16)
    output = lax.all_gather(output_own, MP, axis=0, tiled=True)
    grad_down = scatter_dp(
        jnp.einsum("td,tf->df", cot_rel, active, preferred_element_type=f32).astype(bf16)
    )
    grad_up = scatter_dp(
        jnp.einsum("td,tf->df", second, grad_hidden, preferred_element_type=f32).astype(bf16)
    )

    vec_gain_b = jnp.sum(grad_second * normed_two, axis=0)
    vec_bias_b = jnp.sum(grad_second, axis=0)
    grad_middle = own_cot + norm_back(grad_second, normed_two, inverse_two, gain_b)
    grad_branch = join_blocks(gather_blocks(grad_middle.astype(bf16)))
    grad_out = scatter_dp(
        jnp.einsum("td,tf->df", grad_branch, attended, preferred_element_type=f32).astype(bf16)
    )
    grad_attended = jnp.dot(grad_branch, out_weight, preferred_element_type=f32).astype(bf16)
    grad_attended = to_row_order(grad_attended).reshape(seq_len, local_heads, HEAD_SIZE)
    grad_queries, grad_keys, grad_values = attend_back(
        queries, keys, values, lse, grad_attended, doc_index, scale
    )
    grad_mixed = jnp.concatenate(
        [v.reshape(seq_len, local_width) for v in (grad_queries, grad_keys, grad_values)], axis=1
    ).astype(bf16)
    first_terms = jnp.einsum(
        "tf,df->td", to_relative(grad_mixed), qkv_weight, preferred_element_type=f32
    ).astype(bf16)
    grad_first = scatter_sum(split_blocks(first_terms))
    grad_qkv = scatter_dp(
        jnp.einsum("td,tf->df", first, grad_mixed, preferred_element_type=f32).astype(bf16)
    ).reshape(shard, 3, local_width)

    own_normed, own_inverse = normalize(own_tokens)
    vec_gain_a = jnp.sum(grad_first * own_normed, axis=0)
    vec_bias_a = jnp.sum(grad_first, axis=0)
    grad_tokens = grad_middle + norm_back(grad_first, own_normed, own_inverse, gain_a)
    input_grad = up(to_row_order(join_blocks(gather_blocks(grad_tokens.astype(bf16)))))
    sums = sum_vectors(jnp.stack([vec_gain_a, vec_bias_a, vec_gain_b, vec_bias_b], 0))
    return (
        output,
        input_grad,
        sums[0],
        sums[1],
        grad_qkv,
        grad_out,
        sums[2],
        sums[3],
        grad_up,
        grad_down,
    )


def solution(mesh):
    fine = Mesh(mesh.devices.reshape(NYH, NZ, NC, NX, NYL), ("yh", "z", "c", "x", "yl"))
    return jax.shard_map(
        local,
        mesh=fine,
        in_specs=(
            P(DP, None),
            P(DP, None),
            P(DP),
            P(DP),
            P(DP, None, MP),
            P(DP, MP),
            P(DP),
            P(DP),
            P(DP, MP),
            P(DP, MP),
            P(DP, None),
        ),
        out_specs=(
            P(DP, None),
            P(DP, None),
            P(DP),
            P(DP),
            P(DP, None, MP),
            P(DP, MP),
            P(DP),
            P(DP),
            P(DP, MP),
            P(DP, MP),
        ),
        check_vma=False,
    )
```

```python
import jax
import jax.numpy as jnp
from jax import lax
from jax.experimental import pallas as pl
from jax.experimental.pallas import tpu as pltpu
from jax.sharding import Mesh, PartitionSpec as P

HEAD_SIZE = 128
eps = 1e-05
bf16 = jnp.bfloat16
f32 = jnp.float32

SMALL = pl.CostEstimate(flops=1, bytes_accessed=1, transcendentals=0)

NX, NYL, NZ, NYH, NC = 4, 2, 4, 2, 2
MP = ("x", "yl")
DP = ("yh", "z", "c")
CMP = ("c", "x", "yl")


def up(values):
    return values.astype(f32)


def normalize(values):
    center = values - jnp.mean(values, axis=-1, keepdims=True)
    inverse_std = lax.rsqrt(jnp.mean(center * center, axis=-1, keepdims=True) + eps)
    return (center * inverse_std, inverse_std)


def norm_back(grad_norm, normed, inverse_std, gain):
    scaled = grad_norm * gain
    return inverse_std * (
        scaled
        - jnp.mean(scaled, axis=-1, keepdims=True)
        - normed * jnp.mean(scaled * normed, axis=-1, keepdims=True)
    )


def to_xp(x, y):
    return (x + 1, y)


def to_xm(x, y):
    return (x - 1, y)


def to_y(x, y):
    return (x, y + 1)


def send(values, zero, one):
    pairs = []
    for c in range(NC):
        for x in range(NX):
            for y in range(NYL):
                tx, ty = (zero, one)[c](x, y)
                pairs.append(((c * NX + x) * NYL + y, (c * NX + tx % NX) * NYL + ty % NYL))
    return lax.ppermute(values, CMP, pairs)


def halves(values):
    middle = values.shape[0] // 2
    return values[:middle], values[middle:]


def pick(zero, one):
    return jnp.where(lax.axis_index("c") == 0, zero, one)


def gather_one(own):
    return send(own, to_xp, to_xp), send(own, to_xm, to_xm), send(own, to_y, to_y)


def gather_two(one):
    p1, p2, q = one
    return (
        send(halves(p1)[0], to_xp, to_xp),
        send(halves(p2)[1], to_xm, to_xm),
        send(pick(p1, q), to_y, to_xp),
        send(pick(p2, q), to_y, to_xm),
    )


def gather_three(own, one, two):
    (p1, p2, q), (o1, o2, r1, r2) = one, two
    s1 = send(pick(o1, halves(r1)[0]), to_y, to_xp)
    s2 = send(pick(o2, halves(r2)[1]), to_y, to_xm)
    return {
        (0, 0): (own,),
        (1, 0): (p2,),
        (2, 0): (o1, o2),
        (3, 0): (p1,),
        (0, 1): (q,),
        (1, 1): (r2,),
        (2, 1): (s1, s2),
        (3, 1): (r1,),
    }


STEP_ONE = [(2, 1)]
LATER_STEPS = [(1, 1), (3, 1), (2, 0), (1, 0), (3, 0), (0, 1), (0, 0)]


def core_factors():
    zero = jnp.where(lax.axis_index("c") == 0, 1.0, 0.0).astype(f32)
    return zero, 1.0 - zero


def add_half(block, piece, which, factor):
    first, second = halves(up(block))
    if which == 0:
        first = first + factor * up(piece)
    else:
        second = second + factor * up(piece)
    return jnp.concatenate([first, second], 0)


def scatter_one(blocks):
    h1, h2 = blocks[2, 1]
    return send(h1, to_y, to_xp), send(h2, to_y, to_xm)


def scatter_two(blocks, one):
    zero, single = core_factors()
    s1, s2 = one
    g1, g2 = halves(up(blocks[2, 0]))
    sent = (
        add_half(blocks[1, 1], s1, 0, single).astype(bf16),
        add_half(blocks[3, 1], s2, 1, single).astype(bf16),
        (g1 + zero * up(s1)).astype(bf16),
        (g2 + zero * up(s2)).astype(bf16),
    )
    return (
        send(sent[0], to_y, to_xp),
        send(sent[1], to_y, to_xm),
        send(sent[2], to_xp, to_xp),
        send(sent[3], to_xm, to_xm),
    )


def scatter_three(blocks, two):
    zero, single = core_factors()
    p, q, r1, r2 = two
    u = send((up(blocks[0, 1]) + single * (up(p) + up(q))).astype(bf16), to_y, to_y)
    t1 = send((add_half(blocks[1, 0], r1, 0, 1.0) + zero * up(p)).astype(bf16), to_xp, to_xp)
    t2 = send((add_half(blocks[3, 0], r2, 1, 1.0) + zero * up(q)).astype(bf16), to_xm, to_xm)
    return up(blocks[0, 0]) + up(t1) + up(t2) + up(u)


REL = [(dx, dy) for dy in range(NYL) for dx in range(NX)]
ORDER = [(0, 0), (1, 0), (3, 0), (0, 1), (2, 0), (1, 1), (3, 1), (2, 1)]


def block_index(dx, dy):
    x, y = lax.axis_index("x"), lax.axis_index("yl")
    return ((x + dx) % NX) * NYL + (y + dy) % NYL


def bounce(pieces, starts, rows, dtype=bf16, first_column=0):
    width = pieces[0].shape[1] - first_column
    count = len(pieces)

    def kernel(*refs):
        place_ref, in_refs, out_ref = refs[0], refs[1 : count + 1], refs[count + 1]
        got = refs[count + 2 : 2 * count + 2]
        cast = refs[2 * count + 2 : -2]
        in_sem, out_sem = refs[-2:]
        loads = [
            pltpu.make_async_copy(
                in_refs[k].at[:, pl.ds(first_column, width)], got[k], in_sem.at[k]
            )
            for k in range(count)
        ]
        for load in loads:
            load.start()
        stores = []
        for k in range(count):
            loads[k].wait()
            source = got[k]
            if cast:
                cast[k][...] = got[k][...].astype(dtype)
                source = cast[k]
            begin = pl.multiple_of(place_ref[k], min(16, pieces[k].shape[0]))
            store = pltpu.make_async_copy(
                source, out_ref.at[pl.ds(begin, pieces[k].shape[0])], out_sem.at[k]
            )
            store.start()
            stores.append(store)
        for store in stores:
            store.wait()

    scratch = [pltpu.VMEM((piece.shape[0], width), bf16) for piece in pieces]
    if dtype != bf16:
        scratch += [pltpu.VMEM((piece.shape[0], width), dtype) for piece in pieces]
    return pl.pallas_call(
        kernel,
        out_shape=jax.ShapeDtypeStruct((rows, width), dtype),
        in_specs=[pl.BlockSpec(memory_space=pltpu.SMEM)]
        + [pl.BlockSpec(memory_space=pl.ANY)] * count,
        out_specs=pl.BlockSpec(memory_space=pl.ANY),
        scratch_shapes=scratch
        + [pltpu.SemaphoreType.DMA((count,)), pltpu.SemaphoreType.DMA((count,))],
        compiler_params=pltpu.CompilerParams(vmem_limit_bytes=32 * 2**20),
        cost_estimate=SMALL,
    )(jnp.stack([jnp.asarray(start, jnp.int32) for start in starts]), *pieces)


def assemble(blocks, dtype, first_column=0):
    rows = blocks[0, 0][0].shape[0]
    pieces, starts = [], []
    for key in ORDER:
        begin = block_index(*key) * rows
        for piece in blocks[key]:
            pieces.append(piece)
            starts.append(begin)
            begin = begin + piece.shape[0]
    return bounce(pieces, starts, rows * len(REL), dtype, first_column)


def sum_mp(values):
    copies = jnp.broadcast_to(values[None], (NX * NYL,) + values.shape)
    return jnp.sum(lax.all_to_all(copies, MP, split_axis=0, concat_axis=0, tiled=True), axis=0)


def after(values, *done):
    return lax.optimization_barrier((values,) + done)[0]


def gather_yz(own):
    copies = jnp.broadcast_to(own[None], (NYH * NZ,) + own.shape)
    return lax.all_to_all(copies, ("yh", "z"), split_axis=0, concat_axis=0, tiled=True)


def row_pieces(blocks, rows):
    pieces, starts = [], []
    for i, key in enumerate(REL):
        begin = i * rows
        for piece in blocks[key]:
            pieces.append(piece)
            starts.append(begin)
            begin += piece.shape[0]
    return pieces, starts


def block_places():
    return jnp.stack([block_index(*key) for key in REL]).astype(jnp.int32)


def terms_by_block(keys, parts_of, weight, first=0, relative=False, norm=None):
    seq_len, depth = parts_of[0].shape
    parts, blocks = len(parts_of), len(keys)
    scattered = weight.ndim == 3
    width = weight.shape[0] * weight.shape[1] if scattered else weight.shape[0]
    rows = seq_len // len(REL)
    tile = min(512, width // 4)
    steps = width // tile
    outs = []
    for k, key in enumerate(keys):
        if key == (2, 1):
            outs += [(k, 0, rows // 2), (k, rows // 2, rows // 2)]
        else:
            outs.append((k, 0, rows))

    def kernel(place_ref, *refs):
        lhs_refs = [refs[n * blocks : (n + 1) * blocks] for n in range(parts)]
        w_ref, refs = refs[parts * blocks], refs[parts * blocks + 1 :]
        if norm is not None:
            x_refs, mean_refs, inverse_refs = (
                refs[n * blocks : (n + 1) * blocks] for n in range(3)
            )
            refs = refs[3 * blocks :]
        out_refs, refs = refs[: len(outs)], refs[len(outs) :]
        for part in range(parts):

            @pl.when(pl.program_id(0) // steps == part)
            def _():
                lhs = jnp.concatenate([ref[...] for ref in lhs_refs[part]], 0)
                total = lax.dot_general(
                    lhs,
                    w_ref[...].reshape(tile, depth),
                    (((1,), (1,)), ((), ())),
                    preferred_element_type=f32,
                )
                for out_ref, (k, inside, count) in zip(out_refs, outs):
                    begin = k * rows + inside
                    out_ref[...] = total[begin : begin + count, :].astype(bf16)
                if norm is not None:
                    one = jnp.zeros((1, tile), f32)
                    two = jnp.zeros((1, tile), f32)
                    for k in range(blocks):
                        part_of = total[k * rows : (k + 1) * rows, :]
                        normed = (
                            x_refs[k][...].astype(f32) - mean_refs[k][:, 0:1]
                        ) * inverse_refs[k][:, 0:1]
                        one = one + jnp.sum(part_of * normed, axis=0, keepdims=True)
                        two = two + jnp.sum(part_of, axis=0, keepdims=True)
                    refs[0][0:1, :] = one
                    refs[0][1:2, :] = two

    def rows_spec(k, cols):
        return pl.BlockSpec((rows, cols), lambda j, p: (p[k], 0))

    def tile_spec(k):
        return pl.BlockSpec((rows, tile), lambda j, p: (p[k], j))

    in_specs, operands = [], []
    for lhs in parts_of:
        in_specs += [rows_spec(k, depth) for k in range(blocks)]
        operands += [lhs] * blocks
    if scattered:
        slices, lanes, cols = weight.shape
        half = steps // NYH
        in_specs.append(
            pl.BlockSpec(
                (tile // lanes, 1, lanes, depth),
                lambda j, p: (j % steps % half, j % steps // half, 0, first + j // steps),
            )
        )
        weight = weight.reshape(slices // NYH, NYH, lanes, cols)
    else:
        in_specs.append(pl.BlockSpec((tile, depth), lambda j, p: (j % steps, first + j // steps)))
    operands.append(weight)
    out_specs = [pl.BlockSpec((count, tile), lambda j, p: (0, j)) for _, _, count in outs]
    out_shape = [jax.ShapeDtypeStruct((count, parts * width), bf16) for _, _, count in outs]
    if norm is not None:
        in_specs += [tile_spec(k) for k in range(blocks)]
        in_specs += [rows_spec(k, norm[1].shape[1]) for k in range(blocks)] * 2
        operands += [norm[0]] * blocks + [norm[1]] * blocks + [norm[2]] * blocks
        out_specs.append(pl.BlockSpec((8, tile), lambda j, p: (0, j)))
        out_shape.append(jax.ShapeDtypeStruct((8, width), f32))
    place = jnp.stack(
        [jnp.int32(REL.index(key)) if relative else block_index(*key) for key in keys]
    ).astype(jnp.int32)
    got = pl.pallas_call(
        kernel,
        grid_spec=pltpu.PrefetchScalarGridSpec(
            num_scalar_prefetch=1,
            grid=(parts * steps,),
            in_specs=in_specs,
            out_specs=out_specs,
        ),
        out_shape=out_shape,
        compiler_params=pltpu.CompilerParams(vmem_limit_bytes=48 * 2**20),
        cost_estimate=SMALL,
    )(place, *operands)
    found = {}
    for out, (k, inside, count) in zip(got, outs):
        if keys[k] == (2, 1):
            found.setdefault((2, 1), []).append(out)
        else:
            found[keys[k]] = out
    if norm is not None:
        return found, got[-1]
    return found


def mlp(second, cotangent, weight):
    seq_len, width = cotangent.shape
    rows = seq_len // len(REL)
    slices, lanes, units = weight.shape
    units = units // 2
    weight = weight.reshape(width, 2 * units)
    columns = [
        (n * lanes, ((n % (NZ * NC)) * NYH + n // (NZ * NC)) * lanes) for n in range(slices)
    ]
    tile = min(256, units // 2)
    steps = units // tile
    root, cubic = (2.0 / jnp.pi) ** 0.5, 0.044715
    pieces, starts = row_pieces(second, rows)
    count = len(pieces)

    def kernel(place_ref, *refs):
        cot_ref, down_ref, up_ref, du_ref, z_ref, h_ref, order_ref = refs[count:]

        @pl.when(pl.program_id(0) == 0)
        def _():
            for plain, place in columns:
                for k, start in enumerate(starts):
                    h_ref[start : start + pieces[k].shape[0], place : place + lanes] = refs[k][
                        :, plain : plain + lanes
                    ]
                for i in range(len(REL)):
                    begin = pl.multiple_of(place_ref[i] * rows, rows)
                    order_ref[i * rows : (i + 1) * rows, place : place + lanes] = cot_ref[
                        pl.ds(begin, rows), plain : plain + lanes
                    ]

        u = jnp.dot(h_ref[...], up_ref[...], preferred_element_type=f32)
        dz = jnp.dot(order_ref[...], down_ref[...], preferred_element_type=f32)
        square = u * u
        t = jnp.tanh(root * (u + cubic * (square * u)))
        half = 0.5 * (1.0 + t)
        z_ref[...] = (u * half).astype(bf16)
        slope = half + (0.5 * root) * u * (1.0 - t * t) * (1.0 + (3.0 * cubic) * square)
        du_ref[...] = (dz * slope).astype(bf16)

    whole = lambda shape: pl.BlockSpec(shape, lambda j, p: (0,) * len(shape))
    return pl.pallas_call(
        kernel,
        grid_spec=pltpu.PrefetchScalarGridSpec(
            num_scalar_prefetch=1,
            grid=(steps,),
            in_specs=[whole(piece.shape) for piece in pieces]
            + [
                whole(cotangent.shape),
                pl.BlockSpec((width, tile), lambda j, p: (0, j)),
                pl.BlockSpec((width, tile), lambda j, p: (0, steps + j)),
            ],
            out_specs=[
                pl.BlockSpec((seq_len, tile), lambda j, p: (0, j)),
                pl.BlockSpec((seq_len, tile), lambda j, p: (0, j)),
                whole((seq_len, width)),
            ],
            scratch_shapes=[pltpu.VMEM((seq_len, width), bf16)],
        ),
        out_shape=[
            jax.ShapeDtypeStruct((seq_len, units), bf16),
            jax.ShapeDtypeStruct((seq_len, units), bf16),
            jax.ShapeDtypeStruct((seq_len, width), bf16),
        ],
        compiler_params=pltpu.CompilerParams(vmem_limit_bytes=56 * 2**20),
        cost_estimate=SMALL,
    )(block_places(), *pieces, cotangent, weight, weight)


def mlp_gradients(second, grad_hidden, cotangent, active):
    seq_len, width = second.shape
    rows = seq_len // len(REL)
    cols = active.shape[1]
    slices = NZ * NC
    lanes = width // (slices * NYH)
    tile = NYH * lanes

    def kernel(place_ref, h_ref, du_ref, cot0_ref, cot1_ref, z_ref, out_ref, order_ref):
        @pl.when(pl.program_id(0) == 0)
        def _():
            for i in range(len(REL)):
                begin = pl.multiple_of(place_ref[i] * rows, rows)
                order_ref[pl.ds(begin, rows), :] = z_ref[i * rows : (i + 1) * rows, :]

        over = (((0,), (0,)), ((), ()))
        out_ref[:, :cols] = lax.dot_general(
            h_ref[...], du_ref[...], over, preferred_element_type=f32
        ).astype(bf16)
        cot = jnp.concatenate([cot0_ref[...], cot1_ref[...]], 1)
        out_ref[:, cols:] = lax.dot_general(
            cot, order_ref[...], over, preferred_element_type=f32
        ).astype(bf16)

    near = pl.BlockSpec((seq_len, lanes), lambda i, p: (0, i))
    far = pl.BlockSpec((seq_len, lanes), lambda i, p: (0, slices + i))
    whole = pl.BlockSpec((seq_len, cols), lambda i, p: (0, 0))
    return pl.pallas_call(
        kernel,
        grid_spec=pltpu.PrefetchScalarGridSpec(
            num_scalar_prefetch=1,
            grid=(slices,),
            in_specs=[
                pl.BlockSpec((seq_len, tile), lambda i, p: (0, i)),
                whole,
                near,
                far,
                whole,
            ],
            out_specs=pl.BlockSpec((tile, 2 * cols), lambda i, p: (i, 0)),
            scratch_shapes=[pltpu.VMEM((seq_len, cols), bf16)],
        ),
        out_shape=jax.ShapeDtypeStruct((width, 2 * cols), bf16),
        compiler_params=pltpu.CompilerParams(vmem_limit_bytes=48 * 2**20),
        cost_estimate=SMALL,
    )(block_places(), second, grad_hidden, cotangent, cotangent, active)


def late_gradients(first, grad_mixed, branch, attended, vectors):
    seq_len, width = first.shape
    rows = seq_len // len(REL)
    wide, narrow = grad_mixed.shape[1], attended.shape[1]
    slices = NZ * NC
    part = width // (slices * NYH)
    tile = NYH * part
    lanes = 128
    pieces, starts = row_pieces(branch, rows)
    count = len(pieces)

    def kernel(place_ref, *refs):
        h_ref, mixed_ref, o_ref, vec_ref = refs[:4]
        da_refs = refs[4 : 4 + NYH * count]
        out_ref, lhs_ref, rhs_ref = refs[4 + NYH * count :]

        @pl.when(pl.program_id(0) == 0)
        def _():
            for i in range(len(REL)):
                begin = pl.multiple_of(place_ref[i] * rows, rows)
                rhs_ref[i * rows : (i + 1) * rows, :] = o_ref[pl.ds(begin, rows), :]

        for k, start in enumerate(starts):
            for n in range(NYH):
                lhs_ref[start : start + pieces[k].shape[0], n * part : (n + 1) * part] = da_refs[
                    n * count + k
                ][...]
        over = (((0,), (0,)), ((), ()))
        out_ref[:, :wide] = lax.dot_general(
            h_ref[...], mixed_ref[...], over, preferred_element_type=f32
        ).astype(bf16)
        out_ref[:, wide : wide + narrow] = lax.dot_general(
            lhs_ref[...], rhs_ref[...], over, preferred_element_type=f32
        ).astype(bf16)
        padded = jnp.concatenate([vec_ref[...], jnp.zeros((lanes - 8, tile), f32)], 0)
        out_ref[:, wide + narrow :] = padded.T.astype(bf16)

    whole = lambda shape: pl.BlockSpec(shape, lambda i, p: (0,) * len(shape))
    near = [pl.BlockSpec((piece.shape[0], part), lambda i, p: (0, i)) for piece in pieces]
    far = [pl.BlockSpec((piece.shape[0], part), lambda i, p: (0, slices + i)) for piece in pieces]
    return pl.pallas_call(
        kernel,
        grid_spec=pltpu.PrefetchScalarGridSpec(
            num_scalar_prefetch=1,
            grid=(slices,),
            in_specs=[
                pl.BlockSpec((seq_len, tile), lambda i, p: (0, i)),
                whole(grad_mixed.shape),
                whole(attended.shape),
                pl.BlockSpec((8, tile), lambda i, p: (0, i)),
            ]
            + near
            + far,
            out_specs=pl.BlockSpec((tile, wide + narrow + lanes), lambda i, p: (i, 0)),
            scratch_shapes=[
                pltpu.VMEM((seq_len, tile), bf16),
                pltpu.VMEM((seq_len, narrow), bf16),
            ],
        ),
        out_shape=jax.ShapeDtypeStruct((width, wide + narrow + lanes), bf16),
        compiler_params=pltpu.CompilerParams(vmem_limit_bytes=48 * 2**20),
        cost_estimate=SMALL,
    )(block_places(), first, grad_mixed, attended, vectors, *pieces, *pieces)


def scatter_order(values):
    shape = values.shape
    values = values.reshape(shape[:-1] + (NYH, NZ * NC, -1))
    return jnp.swapaxes(values, -3, -2).reshape(shape)


def pair_yh(own):
    other = lax.ppermute(own, "yh", [(0, 1), (1, 0)])
    first = lax.axis_index("yh") == 0
    return jnp.stack([jnp.where(first, own, other), jnp.where(first, other, own)], 0)


def gather_zc(pair):
    return lax.all_gather(pair, ("z", "c"), axis=0, tiled=True)


def scatter_dp(values):
    values = lax.psum_scatter(values, ("z", "c"), scatter_dimension=0, tiled=True)
    yh = lax.axis_index("yh")
    rows = values.shape[0] // NYH
    home = lax.dynamic_slice_in_dim(values, yh * rows, rows, 0)
    away = lax.dynamic_slice_in_dim(values, (1 - yh) * rows, rows, 0)
    return up(home) + up(lax.ppermute(away, "yh", [(0, 1), (1, 0)]))


def exchange_dp(values):
    rows, cols = values.shape
    values = values.reshape(NZ * NC, NYH, rows // (NZ * NC * NYH), cols)
    values = lax.all_to_all(values, ("z", "c"), split_axis=0, concat_axis=0, tiled=True)
    values = jnp.sum(up(values), axis=0)
    yh = lax.axis_index("yh")
    home = lax.dynamic_index_in_dim(values, yh, 0, keepdims=False)
    away = lax.dynamic_index_in_dim(values, 1 - yh, 0, keepdims=False).astype(bf16)
    return home + up(lax.ppermute(away, "yh", [(0, 1), (1, 0)]))


def norm_and_qkv(tokens, mine, other, cols):
    seq_len, width = tokens.shape
    slices, packed_rows, all_cols = mine.shape
    shard = packed_rows - 16
    tile = min(256, seq_len // 4)

    def kernel(
        place_ref, x_ref, mine_ref, other_ref, h_ref, qkv_ref, w_ref, vec_ref, mean_ref, inverse_ref
    ):
        core = place_ref[0]

        @pl.when(pl.program_id(0) == 0)
        def _():
            for ref, parity in ((mine_ref, core), (other_ref, 1 - core)):
                for s in range(slices):
                    begin = pl.multiple_of((NC * s + parity) * shard, shard)
                    w_ref[pl.ds(begin, shard), :] = ref[s, :shard, :]
                    row = ref[s, shard:, :].astype(f32)
                    for k in range(4):
                        vec_ref[k : k + 1, pl.ds(begin, shard)] = row[
                            0:1, k * shard : (k + 1) * shard
                        ]

        x = x_ref[...].astype(f32)
        mean = jnp.mean(x, axis=-1, keepdims=True)
        center = x - mean
        inverse = lax.rsqrt(jnp.mean(center * center, axis=-1, keepdims=True) + eps)
        mean_ref[...] = jnp.broadcast_to(mean, mean_ref.shape)
        inverse_ref[...] = jnp.broadcast_to(inverse, inverse_ref.shape)
        h = (center * inverse * vec_ref[0:1, :] + vec_ref[1:2, :]).astype(bf16)
        for n in range(NYH * NZ * NC):
            place = (n % (NZ * NC)) * NYH + n // (NZ * NC)
            h_ref[:, place * shard : (place + 1) * shard] = h[:, n * shard : (n + 1) * shard]
        qkv_ref[...] = jnp.dot(h, w_ref[:, :cols], preferred_element_type=f32).astype(bf16)

    whole = lambda shape: pl.BlockSpec(shape, lambda i, p: (0,) * len(shape))
    place = lax.axis_index("c").astype(jnp.int32).reshape(1)
    return pl.pallas_call(
        kernel,
        grid_spec=pltpu.PrefetchScalarGridSpec(
            num_scalar_prefetch=1,
            grid=(seq_len // tile,),
            in_specs=[
                pl.BlockSpec((tile, width), lambda i, p: (i, 0)),
                whole(mine.shape),
                whole(other.shape),
            ],
            out_specs=[
                pl.BlockSpec((tile, width), lambda i, p: (i, 0)),
                pl.BlockSpec((tile, cols), lambda i, p: (i, 0)),
                whole((width, all_cols)),
                whole((8, width)),
                pl.BlockSpec((tile, 128), lambda i, p: (i, 0)),
                pl.BlockSpec((tile, 128), lambda i, p: (i, 0)),
            ],
        ),
        out_shape=[
            jax.ShapeDtypeStruct((seq_len, width), bf16),
            jax.ShapeDtypeStruct((seq_len, cols), bf16),
            jax.ShapeDtypeStruct((width, all_cols), bf16),
            jax.ShapeDtypeStruct((8, width), f32),
            jax.ShapeDtypeStruct((seq_len, 128), f32),
            jax.ShapeDtypeStruct((seq_len, 128), f32),
        ],
        compiler_params=pltpu.CompilerParams(vmem_limit_bytes=48 * 2**20),
        cost_estimate=SMALL,
    )(place, tokens, mine, other)


def scores_of(query, keys, begin, ends_ref, scale):
    rows, seen = query.shape[0], keys.shape[0]
    scores = (
        lax.dot_general(query, keys, (((1,), (1,)), ((), ())), preferred_element_type=f32) * scale
    )
    place = begin + lax.broadcasted_iota(jnp.int32, (rows, 1), 0)
    first = jnp.zeros((rows, 1), jnp.int32)
    for k in range(4):
        first = jnp.where(place >= ends_ref[k], ends_ref[k], first)
    column = lax.broadcasted_iota(jnp.int32, (rows, seen), 1)
    return jnp.where((column >= first) & (column <= place), scores, f32(-1e30))


def attend(qkv, ends, scale):
    seq_len, cols = qkv.shape
    heads = cols // (3 * HEAD_SIZE)
    tile = min(256, seq_len // 4)

    def kernel(ends_ref, q_ref, k_ref, v_ref, o_ref, lse_ref):
        for begin in range(0, seq_len, tile):
            seen = begin + tile
            scores = scores_of(q_ref[begin:seen, :], k_ref[:seen, :], begin, ends_ref, scale)
            largest = jnp.max(scores, axis=-1, keepdims=True)
            expo = jnp.exp(scores - largest)
            totals = jnp.sum(expo, axis=-1, keepdims=True)
            probs = (expo / totals).astype(bf16)
            o_ref[begin:seen, :] = jnp.dot(
                probs, v_ref[:seen, :], preferred_element_type=f32
            ).astype(bf16)
            lse_ref[begin:seen, :] = jnp.broadcast_to(
                largest + jnp.log(totals), (tile, HEAD_SIZE)
            )

    def spec(kind):
        return pl.BlockSpec((seq_len, HEAD_SIZE), lambda h, e: (0, kind * heads + h))

    return pl.pallas_call(
        kernel,
        grid_spec=pltpu.PrefetchScalarGridSpec(
            num_scalar_prefetch=1,
            grid=(heads,),
            in_specs=[spec(0), spec(1), spec(2)],
            out_specs=[spec(0), spec(0)],
        ),
        out_shape=[
            jax.ShapeDtypeStruct((seq_len, heads * HEAD_SIZE), bf16),
            jax.ShapeDtypeStruct((seq_len, heads * HEAD_SIZE), f32),
        ],
        compiler_params=pltpu.CompilerParams(vmem_limit_bytes=48 * 2**20),
        cost_estimate=SMALL,
    )(ends, qkv, qkv, qkv)


def attend_back(qkv, lse, branch, weight, ends, scale):
    seq_len, cols = qkv.shape
    heads = cols // (3 * HEAD_SIZE)
    own = heads * HEAD_SIZE
    width = weight.shape[0]
    rows = seq_len // len(REL)
    tile = min(256, seq_len // 4)
    pieces, starts = row_pieces(branch, rows)
    count = len(pieces)

    def kernel(ends_ref, place_ref, *refs):
        q_ref, k_ref, v_ref, lse_ref, w_ref = refs[:5]
        out_ref, dk_ref, dv_ref, da_ref, go_ref = refs[5 + count :]
        h = pl.program_id(0)

        @pl.when(h == 0)
        def _():
            for k, start in enumerate(starts):
                i, inside = start // rows, start % rows
                begin = pl.multiple_of(place_ref[i] * rows + inside, rows // 2)
                da_ref[pl.ds(begin, pieces[k].shape[0]), :] = refs[5 + k][...]
            grad = jnp.dot(da_ref[...], w_ref[...], preferred_element_type=f32).astype(bf16)
            for n in range(heads):
                go_ref[n] = grad[:, n * HEAD_SIZE : (n + 1) * HEAD_SIZE]

        def columns(kind):
            return pl.ds(pl.multiple_of((kind * heads + h) * HEAD_SIZE, HEAD_SIZE), HEAD_SIZE)

        dk_ref[...] = jnp.zeros_like(dk_ref)
        dv_ref[...] = jnp.zeros_like(dv_ref)
        for begin in range(0, seq_len, tile):
            seen = begin + tile
            query = q_ref[begin:seen, :]
            scores = scores_of(query, k_ref[:seen, :], begin, ends_ref, scale)
            probs = jnp.exp(scores - lse_ref[begin:seen, 0:1])
            grad = go_ref[h, begin:seen, :]
            grad_probs = lax.dot_general(
                grad, v_ref[:seen, :], (((1,), (1,)), ((), ())), preferred_element_type=f32
            )
            inner = jnp.sum(probs * grad_probs, axis=-1, keepdims=True)
            grad_scores = (probs * (grad_probs - inner)).astype(bf16)
            out_ref[begin:seen, columns(0)] = (
                jnp.dot(grad_scores, k_ref[:seen, :], preferred_element_type=f32) * scale
            ).astype(bf16)
            over_rows = (((0,), (0,)), ((), ()))
            dk_ref[:seen, :] += lax.dot_general(
                grad_scores, query, over_rows, preferred_element_type=f32
            )
            dv_ref[:seen, :] += lax.dot_general(
                probs.astype(bf16), grad, over_rows, preferred_element_type=f32
            )
        out_ref[:, columns(1)] = (dk_ref[...] * scale).astype(bf16)
        out_ref[:, columns(2)] = dv_ref[...].astype(bf16)

    def spec(kind):
        return pl.BlockSpec((seq_len, HEAD_SIZE), lambda h, e, p: (0, kind * heads + h))

    whole = lambda shape: pl.BlockSpec(shape, lambda h, e, p: (0,) * len(shape))
    return pl.pallas_call(
        kernel,
        grid_spec=pltpu.PrefetchScalarGridSpec(
            num_scalar_prefetch=2,
            grid=(heads,),
            in_specs=[
                spec(0),
                spec(1),
                spec(2),
                spec(0),
                pl.BlockSpec((width, own), lambda h, e, p: (0, cols // own)),
            ]
            + [whole(piece.shape) for piece in pieces],
            out_specs=whole((seq_len, cols)),
            scratch_shapes=[
                pltpu.VMEM((seq_len, HEAD_SIZE), f32),
                pltpu.VMEM((seq_len, HEAD_SIZE), f32),
                pltpu.VMEM((seq_len, width), bf16),
                pltpu.VMEM((heads, seq_len, HEAD_SIZE), bf16),
            ],
        ),
        out_shape=jax.ShapeDtypeStruct((seq_len, cols), bf16),
        compiler_params=pltpu.CompilerParams(vmem_limit_bytes=56 * 2**20),
        cost_estimate=SMALL,
    )(ends, block_places(), qkv, qkv, qkv, lse, weight, *pieces)


def local(
    tokens,
    doc_lengths,
    gain_one,
    bias_one,
    w_qkv,
    w_out,
    gain_two,
    bias_two,
    w_up,
    w_down,
    cotangent,
):
    seq_len, width = tokens.shape
    shard = w_qkv.shape[0]
    local_width = w_qkv.shape[2]
    local_heads = local_width // HEAD_SIZE
    rows = seq_len // (NX * NYL)
    x, y = lax.axis_index("x"), lax.axis_index("yl")
    my_rows = (x * NYL + y) * rows
    scale = HEAD_SIZE**-0.5

    wide = 3 * local_width
    small = jnp.stack([gain_one, bias_one, gain_two, bias_two], 0).astype(bf16)
    small = jnp.pad(small.reshape(1, -1), ((0, 15), (0, wide + local_width - 4 * shard)))
    packed = jnp.concatenate([w_qkv.reshape(shard, wide).astype(bf16), w_out.astype(bf16)], 1)
    first_mine = gather_yz(jnp.concatenate([packed, small], 0))
    first_other = lax.ppermute(first_mine, "c", [(0, 1), (1, 0)])
    mlp_weight = jnp.concatenate([w_down.astype(bf16), w_up.astype(bf16)], 1)
    mlp_weight = gather_zc(pair_yh(after(mlp_weight, first_mine)))
    ends = jnp.cumsum(doc_lengths[0])

    first, mixed, weight, vectors, mean_one, inverse_one = norm_and_qkv(
        tokens, first_mine, first_other, wide
    )
    gain_a, gain_b, bias_b = vectors[0], vectors[2], vectors[3]
    attended, lse = attend(mixed, ends, scale)
    terms = terms_by_block(STEP_ONE, [attended], weight, first=3)
    sum_one = scatter_one(terms)
    later = terms_by_block(LATER_STEPS, [after(attended, *terms[2, 1])], weight, first=3)
    own_tokens = up(lax.dynamic_slice_in_dim(tokens, my_rows, rows, 0))
    own_cot = up(lax.dynamic_slice_in_dim(cotangent, my_rows, rows, 0))
    own_middle = own_tokens + scatter_three(later, scatter_two(later, sum_one))

    own_two, inverse_two = normalize(own_middle)
    second = (own_two * gain_b + bias_b).astype(bf16)
    second_one = gather_one(second)
    second_two = gather_two(second_one)
    grad_hidden, active, second = mlp(
        gather_three(second, second_one, second_two), cotangent, mlp_weight
    )
    hidden = [active, grad_hidden]
    terms = terms_by_block(STEP_ONE, hidden, mlp_weight, relative=True)
    sum_one = scatter_one(terms)
    later = terms_by_block(
        LATER_STEPS, after(hidden, *terms[2, 1]), mlp_weight, relative=True
    )
    sum_two = scatter_two(later, sum_one)
    both = scatter_three(later, sum_two)
    mlp_terms = mlp_gradients(after(second, sum_two[2]), grad_hidden, cotangent, active)
    both = after(both, mlp_terms)
    mlp_grads = scatter_dp(mlp_terms)
    branch_two, grad_second = both[:, :width], both[:, width:]
    output_own = (own_middle + branch_two).astype(bf16)

    grad_middle = own_cot + norm_back(grad_second, own_two, inverse_two, gain_b)
    own_branch = grad_middle.astype(bf16)
    branch_one = gather_one(own_branch)
    branch_two = gather_two(branch_one)
    branch = gather_three(own_branch, branch_one, branch_two)
    output_one = gather_one(after(output_own, branch_two[0]))
    grad_mixed = attend_back(mixed, lse, branch, weight, ends, scale)
    norm = (tokens, mean_one, inverse_one)
    terms, vec_a = terms_by_block(STEP_ONE, [grad_mixed], weight, norm=norm)
    sum_one = scatter_one(terms)
    output_two = gather_two(output_one)
    later, vec_b = terms_by_block(
        LATER_STEPS, [after(grad_mixed, *terms[2, 1])], weight, norm=norm
    )
    sum_two = scatter_two(later, sum_one)
    vec_one = vec_a + vec_b
    vec_two = jnp.stack([jnp.sum(grad_second * own_two, 0), jnp.sum(grad_second, 0)], 0)
    late_vectors = scatter_order(
        jnp.concatenate([vec_one[:2], vec_two, jnp.zeros((4, width), f32)], 0)
    )
    output_two = after(output_two, *sum_two)
    grad_first = scatter_three(later, sum_two)
    late = exchange_dp(
        late_gradients(after(first, sum_two[2]), grad_mixed, branch, attended, late_vectors)
    )

    own_one, own_inverse = normalize(own_tokens)
    grad_tokens = (grad_middle + norm_back(grad_first, own_one, own_inverse, gain_a)).astype(bf16)
    grad_one = gather_one(grad_tokens)
    grad_two = after(gather_two(grad_one), late)
    output = gather_three(output_own, output_one, output_two)
    output = assemble(after(output, *grad_two), bf16)
    input_grad = assemble(gather_three(grad_tokens, grad_one, grad_two), f32)
    sums = sum_mp(late[:, wide + local_width : wide + local_width + 4].T)
    return (
        output,
        input_grad,
        sums[0],
        sums[1],
        late[:, :wide].reshape(shard, 3, local_width),
        late[:, wide : wide + local_width],
        sums[2],
        sums[3],
        mlp_grads[:, : w_up.shape[1]],
        mlp_grads[:, w_up.shape[1] :],
    )


def solution(mesh):
    fine = Mesh(mesh.devices.reshape(NYH, NZ, NC, NX, NYL), ("yh", "z", "c", "x", "yl"))
    return jax.shard_map(
        local,
        mesh=fine,
        in_specs=(
            P(DP, None),
            P(DP, None),
            P(DP),
            P(DP),
            P(DP, None, MP),
            P(DP, MP),
            P(DP),
            P(DP),
            P(DP, MP),
            P(DP, MP),
            P(DP, None),
        ),
        out_specs=(
            P(DP, None),
            P(DP, None),
            P(DP),
            P(DP),
            P(DP, None, MP),
            P(DP, MP),
            P(DP),
            P(DP),
            P(DP, MP),
            P(DP, MP),
        ),
        check_vma=False,
    )
```

```python
import jax
import jax.numpy as jnp
from jax import lax
from jax.experimental import pallas as pl
from jax.experimental.pallas import tpu as pltpu
from jax.sharding import Mesh, PartitionSpec as P

HEAD_SIZE = 128
eps = 1e-05
bf16 = jnp.bfloat16
f32 = jnp.float32

SMALL = pl.CostEstimate(flops=1, bytes_accessed=1, transcendentals=0)


def cost(micros):
    return pl.CostEstimate(
        flops=int(micros * 1.1e9), bytes_accessed=int(micros * 3.0e6), transcendentals=0
    )


NX, NYL, NZ, NYH, NC = 4, 2, 4, 2, 2
MP = ("x", "yl")
DP = ("yh", "z", "c")
CMP = ("c", "x", "yl")


def up(values):
    return values.astype(f32)


def normalize(values):
    center = values - jnp.mean(values, axis=-1, keepdims=True)
    inverse_std = lax.rsqrt(jnp.mean(center * center, axis=-1, keepdims=True) + eps)
    return (center * inverse_std, inverse_std)


def norm_back(grad_norm, normed, inverse_std, gain):
    scaled = grad_norm * gain
    return inverse_std * (
        scaled
        - jnp.mean(scaled, axis=-1, keepdims=True)
        - normed * jnp.mean(scaled * normed, axis=-1, keepdims=True)
    )


def to_xp(x, y):
    return (x + 1, y)


def to_xm(x, y):
    return (x - 1, y)


def to_y(x, y):
    return (x, y + 1)


def send(values, zero, one):
    pairs = []
    for c in range(NC):
        for x in range(NX):
            for y in range(NYL):
                tx, ty = (zero, one)[c](x, y)
                pairs.append(((c * NX + x) * NYL + y, (c * NX + tx % NX) * NYL + ty % NYL))
    return lax.ppermute(values, CMP, pairs)


def halves(values):
    middle = values.shape[0] // 2
    return values[:middle], values[middle:]


def gather_one(own):
    return send(own, to_xp, to_xp), send(own, to_xm, to_xm), send(own, to_y, to_y)


def columnwise(body, ins, out_rows):
    width = ins[0].shape[1]
    tile = min(1024, width)

    def kernel(core_ref, *refs):
        outs = body(core_ref[0], [ref[...] for ref in refs[: len(ins)]])
        for ref, out in zip(refs[len(ins) :], outs):
            ref[...] = out.astype(bf16)

    return pl.pallas_call(
        kernel,
        grid_spec=pltpu.PrefetchScalarGridSpec(
            num_scalar_prefetch=1,
            grid=(width // tile,),
            in_specs=[pl.BlockSpec((v.shape[0], tile), lambda j, c: (0, j)) for v in ins],
            out_specs=[pl.BlockSpec((rows, tile), lambda j, c: (0, j)) for rows in out_rows],
        ),
        out_shape=[jax.ShapeDtypeStruct((rows, width), bf16) for rows in out_rows],
        compiler_params=pltpu.CompilerParams(vmem_limit_bytes=16 * 2**20),
        cost_estimate=SMALL,
    )(lax.axis_index("c").astype(jnp.int32).reshape(1), *ins)


def gather_two(one):
    p1, p2, q = one
    rows = q.shape[0]

    def body(core, values):
        p1, p2, q = values
        return (
            halves(p1)[0],
            halves(p2)[1],
            jnp.where(core == 0, p1, q),
            jnp.where(core == 0, p2, q),
        )

    o1, o2, r1, r2 = columnwise(body, one, [rows // 2, rows // 2, rows, rows])
    return (
        send(o1, to_xp, to_xp),
        send(o2, to_xm, to_xm),
        send(r1, to_y, to_xp),
        send(r2, to_y, to_xm),
    )


def gather_three(own, one, two):
    (p1, p2, q), (o1, o2, r1, r2) = one, two
    half = o1.shape[0]

    def body(core, values):
        o1, o2, r1, r2 = values
        return (
            jnp.where(core == 0, o1, halves(r1)[0]),
            jnp.where(core == 0, o2, halves(r2)[1]),
        )

    s1, s2 = columnwise(body, two, [half, half])
    s1 = send(s1, to_y, to_xp)
    s2 = send(s2, to_y, to_xm)
    return {
        (0, 0): (own,),
        (1, 0): (p2,),
        (2, 0): (o1, o2),
        (3, 0): (p1,),
        (0, 1): (q,),
        (1, 1): (r2,),
        (2, 1): (s1, s2),
        (3, 1): (r1,),
    }


STEP_ONE = [(2, 1)]
LATER_STEPS = [(1, 1), (3, 1), (2, 0), (1, 0), (3, 0), (0, 1), (0, 0)]


def core_factors(core):
    zero = jnp.where(core == 0, 1.0, 0.0).astype(f32)
    return zero, 1.0 - zero


def scatter_one(blocks):
    h1, h2 = blocks[2, 1]
    return send(h1, to_y, to_xp), send(h2, to_y, to_xm)


def scatter_two(blocks, one):
    rows = blocks[2, 0].shape[0]

    def body(core, values):
        zero, single = core_factors(core)
        b1, b3, b2, s1, s2 = (up(v) for v in values)
        first, second = halves(b1)
        third, fourth = halves(b3)
        g1, g2 = halves(b2)
        return (
            jnp.concatenate([first + single * s1, second], 0),
            jnp.concatenate([third, fourth + single * s2], 0),
            g1 + zero * s1,
            g2 + zero * s2,
        )

    p, q, r1, r2 = columnwise(
        body,
        [blocks[1, 1], blocks[3, 1], blocks[2, 0], *one],
        [rows, rows, rows // 2, rows // 2],
    )
    return (
        send(p, to_y, to_xp),
        send(q, to_y, to_xm),
        send(r1, to_xp, to_xp),
        send(r2, to_xm, to_xm),
    )


def scatter_three(blocks, two):
    rows = blocks[0, 0].shape[0]

    def body(core, values):
        zero, single = core_factors(core)
        b1, b3, b0, p, q, r1, r2 = (up(v) for v in values)
        first, second = halves(b1 + zero * p)
        third, fourth = halves(b3 + zero * q)
        return (
            jnp.concatenate([first + r1, second], 0),
            jnp.concatenate([third, fourth + r2], 0),
            b0 + single * (p + q),
        )

    t1, t2, u = columnwise(
        body, [blocks[1, 0], blocks[3, 0], blocks[0, 1], *two], [rows, rows, rows]
    )
    t1 = send(t1, to_xp, to_xp)
    t2 = send(t2, to_xm, to_xm)
    u = send(u, to_y, to_y)
    return up(blocks[0, 0]) + up(t1) + up(t2) + up(u)


REL = [(dx, dy) for dy in range(NYL) for dx in range(NX)]
ORDER = [(0, 0), (1, 0), (3, 0), (0, 1), (2, 0), (1, 1), (3, 1), (2, 1)]


def block_index(dx, dy):
    x, y = lax.axis_index("x"), lax.axis_index("yl")
    return ((x + dx) % NX) * NYL + (y + dy) % NYL


def bounce(pieces, starts, rows, width, dtype, first_column):
    count = len(pieces)

    def kernel(*refs):
        place_ref, in_refs, out_ref = refs[0], refs[1 : count + 1], refs[count + 1]
        got = refs[count + 2 : 2 * count + 2]
        cast = refs[2 * count + 2 : -2]
        in_sem, out_sem = refs[-2:]
        loads = [
            pltpu.make_async_copy(
                in_refs[k].at[:, pl.ds(first_column, width)], got[k], in_sem.at[k]
            )
            for k in range(count)
        ]
        for load in loads:
            load.start()
        stores = []
        for k in range(count):
            loads[k].wait()
            source = got[k]
            if cast:
                cast[k][...] = got[k][...].astype(dtype)
                source = cast[k]
            begin = pl.multiple_of(place_ref[k], min(16, pieces[k].shape[0]))
            store = pltpu.make_async_copy(
                source, out_ref.at[pl.ds(begin, pieces[k].shape[0])], out_sem.at[k]
            )
            store.start()
            stores.append(store)
        for store in stores:
            store.wait()

    scratch = [pltpu.VMEM((piece.shape[0], width), bf16) for piece in pieces]
    if dtype != bf16:
        scratch += [pltpu.VMEM((piece.shape[0], width), dtype) for piece in pieces]
    return pl.pallas_call(
        kernel,
        out_shape=jax.ShapeDtypeStruct((rows, width), dtype),
        in_specs=[pl.BlockSpec(memory_space=pltpu.SMEM)]
        + [pl.BlockSpec(memory_space=pl.ANY)] * count,
        out_specs=pl.BlockSpec(memory_space=pl.ANY),
        scratch_shapes=scratch
        + [pltpu.SemaphoreType.DMA((count,)), pltpu.SemaphoreType.DMA((count,))],
        compiler_params=pltpu.CompilerParams(vmem_limit_bytes=20 * 2**20),
        cost_estimate=SMALL,
    )(jnp.stack([jnp.asarray(start, jnp.int32) for start in starts]), *pieces)


def assemble(blocks, width, dtype, first_column):
    rows = blocks[0, 0][0].shape[0]
    pieces, starts = [], []
    for key in ORDER:
        begin = block_index(*key) * rows
        for piece in blocks[key]:
            pieces.append(piece)
            starts.append(begin)
            begin = begin + piece.shape[0]
    return bounce(pieces, starts, rows * len(REL), width, dtype, first_column)


def sum_mp(values):
    copies = jnp.broadcast_to(values[None], (NX * NYL,) + values.shape)
    return jnp.sum(lax.all_to_all(copies, MP, split_axis=0, concat_axis=0, tiled=True), axis=0)


def after(values, *done):
    return lax.optimization_barrier((values,) + done)[0]


def gather_yz(own):
    copies = jnp.broadcast_to(own[None], (NYH * NZ,) + own.shape)
    return lax.all_to_all(copies, ("yh", "z"), split_axis=0, concat_axis=0, tiled=True)


def row_pieces(blocks, rows):
    pieces, starts = [], []
    for i, key in enumerate(REL):
        begin = i * rows
        for piece in blocks[key]:
            pieces.append(piece)
            starts.append(begin)
            begin += piece.shape[0]
    return pieces, starts


def block_places():
    return jnp.stack([block_index(*key) for key in REL]).astype(jnp.int32)


def terms_by_block(keys, parts_of, weight, first=0, relative=False, norm=None):
    seq_len, depth = parts_of[0].shape
    parts, blocks = len(parts_of), len(keys)
    scattered = weight.ndim == 3
    width = weight.shape[0] * weight.shape[1] if scattered else weight.shape[0]
    rows = seq_len // len(REL)
    tile = min(512, width // 4)
    steps = width // tile
    outs = []
    for k, key in enumerate(keys):
        if key == (2, 1):
            outs += [(k, 0, rows // 2), (k, rows // 2, rows // 2)]
        else:
            outs.append((k, 0, rows))

    def kernel(place_ref, *refs):
        lhs_refs = [refs[n * blocks : (n + 1) * blocks] for n in range(parts)]
        w_ref, refs = refs[parts * blocks], refs[parts * blocks + 1 :]
        if norm is not None:
            x_refs, mean_refs, inverse_refs = (
                refs[n * blocks : (n + 1) * blocks] for n in range(3)
            )
            refs = refs[3 * blocks :]
        out_refs, refs = refs[: len(outs)], refs[len(outs) :]
        for part in range(parts):

            @pl.when(pl.program_id(0) // steps == part)
            def _():
                lhs = jnp.concatenate([ref[...] for ref in lhs_refs[part]], 0)
                total = lax.dot_general(
                    lhs,
                    w_ref[...].reshape(tile, depth),
                    (((1,), (1,)), ((), ())),
                    preferred_element_type=f32,
                )
                for out_ref, (k, inside, count) in zip(out_refs, outs):
                    begin = k * rows + inside
                    out_ref[...] = total[begin : begin + count, :].astype(bf16)
                if norm is not None:
                    one = jnp.zeros((1, tile), f32)
                    two = jnp.zeros((1, tile), f32)
                    for k in range(blocks):
                        part_of = total[k * rows : (k + 1) * rows, :]
                        normed = (
                            x_refs[k][...].astype(f32) - mean_refs[k][:, 0:1]
                        ) * inverse_refs[k][:, 0:1]
                        one = one + jnp.sum(part_of * normed, axis=0, keepdims=True)
                        two = two + jnp.sum(part_of, axis=0, keepdims=True)
                    refs[0][0:1, :] = one
                    refs[0][1:2, :] = two

    def rows_spec(k, cols):
        return pl.BlockSpec((rows, cols), lambda j, p: (p[k], 0))

    def tile_spec(k):
        return pl.BlockSpec((rows, tile), lambda j, p: (p[k], j))

    in_specs, operands = [], []
    for lhs in parts_of:
        in_specs += [rows_spec(k, depth) for k in range(blocks)]
        operands += [lhs] * blocks
    if scattered:
        slices, lanes, cols = weight.shape
        half = steps // NYH
        in_specs.append(
            pl.BlockSpec(
                (tile // lanes, 1, lanes, depth),
                lambda j, p: (j % steps % half, j % steps // half, 0, first + j // steps),
            )
        )
        weight = weight.reshape(slices // NYH, NYH, lanes, cols)
    else:
        in_specs.append(pl.BlockSpec((tile, depth), lambda j, p: (j % steps, first + j // steps)))
    operands.append(weight)
    out_specs = [pl.BlockSpec((count, tile), lambda j, p: (0, j)) for _, _, count in outs]
    out_shape = [jax.ShapeDtypeStruct((count, parts * width), bf16) for _, _, count in outs]
    if norm is not None:
        in_specs += [tile_spec(k) for k in range(blocks)]
        in_specs += [rows_spec(k, norm[1].shape[1]) for k in range(blocks)] * 2
        operands += [norm[0]] * blocks + [norm[1]] * blocks + [norm[2]] * blocks
        out_specs.append(pl.BlockSpec((8, tile), lambda j, p: (0, j)))
        out_shape.append(jax.ShapeDtypeStruct((8, width), f32))
    place = jnp.stack(
        [jnp.int32(REL.index(key)) if relative else block_index(*key) for key in keys]
    ).astype(jnp.int32)
    got = pl.pallas_call(
        kernel,
        grid_spec=pltpu.PrefetchScalarGridSpec(
            num_scalar_prefetch=1,
            grid=(parts * steps,),
            in_specs=in_specs,
            out_specs=out_specs,
        ),
        out_shape=out_shape,
        compiler_params=pltpu.CompilerParams(vmem_limit_bytes=28 * 2**20),
        cost_estimate=cost(1 + blocks),
    )(place, *operands)
    found = {}
    for out, (k, inside, count) in zip(got, outs):
        if keys[k] == (2, 1):
            found.setdefault((2, 1), []).append(out)
        else:
            found[keys[k]] = out
    if norm is not None:
        return found, got[-1]
    return found


def mlp(second, cotangent, weight):
    seq_len, width = cotangent.shape
    rows = seq_len // len(REL)
    slices, lanes, units = weight.shape
    units = units // 2
    weight = weight.reshape(width, 2 * units)
    columns = [
        (n * lanes, ((n % (NZ * NC)) * NYH + n // (NZ * NC)) * lanes) for n in range(slices)
    ]
    tile = min(256, units // 2)
    steps = units // tile
    root, cubic = (2.0 / jnp.pi) ** 0.5, 0.044715
    pieces, starts = row_pieces(second, rows)
    count = len(pieces)

    def kernel(place_ref, *refs):
        cot_ref, down_ref, up_ref, du_ref, z_ref, h_ref, order_ref = refs[count:]

        @pl.when(pl.program_id(0) == 0)
        def _():
            for plain, place in columns:
                for k, start in enumerate(starts):
                    h_ref[start : start + pieces[k].shape[0], place : place + lanes] = refs[k][
                        :, plain : plain + lanes
                    ]
                for i in range(len(REL)):
                    begin = pl.multiple_of(place_ref[i] * rows, rows)
                    order_ref[i * rows : (i + 1) * rows, place : place + lanes] = cot_ref[
                        pl.ds(begin, rows), plain : plain + lanes
                    ]

        u = jnp.dot(h_ref[...], up_ref[...], preferred_element_type=f32)
        dz = jnp.dot(order_ref[...], down_ref[...], preferred_element_type=f32)
        square = u * u
        t = jnp.tanh(root * (u + cubic * (square * u)))
        half = 0.5 * (1.0 + t)
        z_ref[...] = (u * half).astype(bf16)
        slope = half + (0.5 * root) * u * (1.0 - t * t) * (1.0 + (3.0 * cubic) * square)
        du_ref[...] = (dz * slope).astype(bf16)

    whole = lambda shape: pl.BlockSpec(shape, lambda j, p: (0,) * len(shape))
    return pl.pallas_call(
        kernel,
        grid_spec=pltpu.PrefetchScalarGridSpec(
            num_scalar_prefetch=1,
            grid=(steps,),
            in_specs=[whole(piece.shape) for piece in pieces]
            + [
                whole(cotangent.shape),
                pl.BlockSpec((width, tile), lambda j, p: (0, j)),
                pl.BlockSpec((width, tile), lambda j, p: (0, steps + j)),
            ],
            out_specs=[
                pl.BlockSpec((seq_len, tile), lambda j, p: (0, j)),
                pl.BlockSpec((seq_len, tile), lambda j, p: (0, j)),
                whole((seq_len, width)),
            ],
            scratch_shapes=[pltpu.VMEM((seq_len, width), bf16)],
        ),
        out_shape=[
            jax.ShapeDtypeStruct((seq_len, units), bf16),
            jax.ShapeDtypeStruct((seq_len, units), bf16),
            jax.ShapeDtypeStruct((seq_len, width), bf16),
        ],
        compiler_params=pltpu.CompilerParams(vmem_limit_bytes=48 * 2**20),
        cost_estimate=cost(18),
    )(block_places(), *pieces, cotangent, weight, weight)


def mlp_gradients(second, grad_hidden, cotangent, active):
    seq_len, width = second.shape
    rows = seq_len // len(REL)
    cols = active.shape[1]
    slices = NZ * NC
    lanes = width // (slices * NYH)
    tile = NYH * lanes

    def kernel(place_ref, h_ref, du_ref, cot0_ref, cot1_ref, z_ref, out_ref, order_ref):
        @pl.when(pl.program_id(0) == 0)
        def _():
            for i in range(len(REL)):
                begin = pl.multiple_of(place_ref[i] * rows, rows)
                order_ref[pl.ds(begin, rows), :] = z_ref[i * rows : (i + 1) * rows, :]

        over = (((0,), (0,)), ((), ()))
        out_ref[:, :cols] = lax.dot_general(
            h_ref[...], du_ref[...], over, preferred_element_type=f32
        ).astype(bf16)
        cot = jnp.concatenate([cot0_ref[...], cot1_ref[...]], 1)
        out_ref[:, cols:] = lax.dot_general(
            cot, order_ref[...], over, preferred_element_type=f32
        ).astype(bf16)

    near = pl.BlockSpec((seq_len, lanes), lambda i, p: (0, i))
    far = pl.BlockSpec((seq_len, lanes), lambda i, p: (0, slices + i))
    whole = pl.BlockSpec((seq_len, cols), lambda i, p: (0, 0))
    return pl.pallas_call(
        kernel,
        grid_spec=pltpu.PrefetchScalarGridSpec(
            num_scalar_prefetch=1,
            grid=(slices,),
            in_specs=[
                pl.BlockSpec((seq_len, tile), lambda i, p: (0, i)),
                whole,
                near,
                far,
                whole,
            ],
            out_specs=pl.BlockSpec((tile, 2 * cols), lambda i, p: (i, 0)),
            scratch_shapes=[pltpu.VMEM((seq_len, cols), bf16)],
        ),
        out_shape=jax.ShapeDtypeStruct((width, 2 * cols), bf16),
        compiler_params=pltpu.CompilerParams(vmem_limit_bytes=24 * 2**20),
        cost_estimate=cost(14),
    )(block_places(), second, grad_hidden, cotangent, cotangent, active)


def late_gradients(first, grad_mixed, branch, attended, vectors):
    seq_len, width = first.shape
    rows = seq_len // len(REL)
    wide, narrow = grad_mixed.shape[1], attended.shape[1]
    slices = NZ * NC
    part = width // (slices * NYH)
    tile = NYH * part
    lanes = 128
    pieces, starts = row_pieces(branch, rows)
    count = len(pieces)

    def kernel(place_ref, *refs):
        h_ref, mixed_ref, o_ref, vec_ref = refs[:4]
        da_refs = refs[4 : 4 + NYH * count]
        out_ref, lhs_ref, rhs_ref = refs[4 + NYH * count :]

        @pl.when(pl.program_id(0) == 0)
        def _():
            for i in range(len(REL)):
                begin = pl.multiple_of(place_ref[i] * rows, rows)
                rhs_ref[i * rows : (i + 1) * rows, :] = o_ref[pl.ds(begin, rows), :]

        for k, start in enumerate(starts):
            for n in range(NYH):
                lhs_ref[start : start + pieces[k].shape[0], n * part : (n + 1) * part] = da_refs[
                    n * count + k
                ][...]
        over = (((0,), (0,)), ((), ()))
        out_ref[:, :wide] = lax.dot_general(
            h_ref[...], mixed_ref[...], over, preferred_element_type=f32
        ).astype(bf16)
        out_ref[:, wide : wide + narrow] = lax.dot_general(
            lhs_ref[...], rhs_ref[...], over, preferred_element_type=f32
        ).astype(bf16)
        padded = jnp.concatenate([vec_ref[...], jnp.zeros((lanes - 8, tile), f32)], 0)
        out_ref[:, wide + narrow :] = padded.T.astype(bf16)

    whole = lambda shape: pl.BlockSpec(shape, lambda i, p: (0,) * len(shape))
    near = [pl.BlockSpec((piece.shape[0], part), lambda i, p: (0, i)) for piece in pieces]
    far = [pl.BlockSpec((piece.shape[0], part), lambda i, p: (0, slices + i)) for piece in pieces]
    return pl.pallas_call(
        kernel,
        grid_spec=pltpu.PrefetchScalarGridSpec(
            num_scalar_prefetch=1,
            grid=(slices,),
            in_specs=[
                pl.BlockSpec((seq_len, tile), lambda i, p: (0, i)),
                whole(grad_mixed.shape),
                whole(attended.shape),
                pl.BlockSpec((8, tile), lambda i, p: (0, i)),
            ]
            + near
            + far,
            out_specs=pl.BlockSpec((tile, wide + narrow + lanes), lambda i, p: (i, 0)),
            scratch_shapes=[
                pltpu.VMEM((seq_len, tile), bf16),
                pltpu.VMEM((seq_len, narrow), bf16),
            ],
        ),
        out_shape=jax.ShapeDtypeStruct((width, wide + narrow + lanes), bf16),
        compiler_params=pltpu.CompilerParams(vmem_limit_bytes=24 * 2**20),
        cost_estimate=cost(11),
    )(block_places(), first, grad_mixed, attended, vectors, *pieces, *pieces)


def scatter_order(values):
    shape = values.shape
    values = values.reshape(shape[:-1] + (NYH, NZ * NC, -1))
    return jnp.swapaxes(values, -3, -2).reshape(shape)


def pair_yh(own):
    other = lax.ppermute(own, "yh", [(0, 1), (1, 0)])
    first = lax.axis_index("yh") == 0
    return jnp.stack([jnp.where(first, own, other), jnp.where(first, other, own)], 0)


def gather_zc(pair):
    return lax.all_gather(pair, ("z", "c"), axis=0, tiled=True)


def scatter_dp(values):
    values = lax.psum_scatter(values, ("z", "c"), scatter_dimension=0, tiled=True)
    yh = lax.axis_index("yh")
    rows = values.shape[0] // NYH
    home = lax.dynamic_slice_in_dim(values, yh * rows, rows, 0)
    away = lax.dynamic_slice_in_dim(values, (1 - yh) * rows, rows, 0)
    return up(home) + up(lax.ppermute(away, "yh", [(0, 1), (1, 0)]))


def norm_and_qkv(tokens, mine, other, cols):
    seq_len, width = tokens.shape
    slices, packed_rows, all_cols = mine.shape
    shard = packed_rows - 16
    tile = min(256, seq_len // 4)

    def kernel(
        place_ref, x_ref, mine_ref, other_ref, h_ref, qkv_ref, w_ref, vec_ref, mean_ref, inverse_ref
    ):
        core = place_ref[0]

        @pl.when(pl.program_id(0) == 0)
        def _():
            for ref, parity in ((mine_ref, core), (other_ref, 1 - core)):
                for s in range(slices):
                    begin = pl.multiple_of((NC * s + parity) * shard, shard)
                    w_ref[pl.ds(begin, shard), :] = ref[s, :shard, :]
                    row = ref[s, shard:, :].astype(f32)
                    for k in range(4):
                        vec_ref[k : k + 1, pl.ds(begin, shard)] = row[
                            0:1, k * shard : (k + 1) * shard
                        ]

        x = x_ref[...].astype(f32)
        mean = jnp.mean(x, axis=-1, keepdims=True)
        center = x - mean
        inverse = lax.rsqrt(jnp.mean(center * center, axis=-1, keepdims=True) + eps)
        mean_ref[...] = jnp.broadcast_to(mean, mean_ref.shape)
        inverse_ref[...] = jnp.broadcast_to(inverse, inverse_ref.shape)
        h = (center * inverse * vec_ref[0:1, :] + vec_ref[1:2, :]).astype(bf16)
        for n in range(NYH * NZ * NC):
            place = (n % (NZ * NC)) * NYH + n // (NZ * NC)
            h_ref[:, place * shard : (place + 1) * shard] = h[:, n * shard : (n + 1) * shard]
        qkv_ref[...] = jnp.dot(h, w_ref[:, :cols], preferred_element_type=f32).astype(bf16)

    whole = lambda shape: pl.BlockSpec(shape, lambda i, p: (0,) * len(shape))
    place = lax.axis_index("c").astype(jnp.int32).reshape(1)
    return pl.pallas_call(
        kernel,
        grid_spec=pltpu.PrefetchScalarGridSpec(
            num_scalar_prefetch=1,
            grid=(seq_len // tile,),
            in_specs=[
                pl.BlockSpec((tile, width), lambda i, p: (i, 0)),
                whole(mine.shape),
                whole(other.shape),
            ],
            out_specs=[
                pl.BlockSpec((tile, width), lambda i, p: (i, 0)),
                pl.BlockSpec((tile, cols), lambda i, p: (i, 0)),
                whole((width, all_cols)),
                whole((8, width)),
                pl.BlockSpec((tile, 128), lambda i, p: (i, 0)),
                pl.BlockSpec((tile, 128), lambda i, p: (i, 0)),
            ],
        ),
        out_shape=[
            jax.ShapeDtypeStruct((seq_len, width), bf16),
            jax.ShapeDtypeStruct((seq_len, cols), bf16),
            jax.ShapeDtypeStruct((width, all_cols), bf16),
            jax.ShapeDtypeStruct((8, width), f32),
            jax.ShapeDtypeStruct((seq_len, 128), f32),
            jax.ShapeDtypeStruct((seq_len, 128), f32),
        ],
        compiler_params=pltpu.CompilerParams(vmem_limit_bytes=36 * 2**20),
        cost_estimate=cost(9),
    )(place, tokens, mine, other)


def scores_of(query, keys, begin, ends_ref, scale):
    rows, seen = query.shape[0], keys.shape[0]
    scores = (
        lax.dot_general(query, keys, (((1,), (1,)), ((), ())), preferred_element_type=f32) * scale
    )
    place = begin + lax.broadcasted_iota(jnp.int32, (rows, 1), 0)
    first = jnp.zeros((rows, 1), jnp.int32)
    for k in range(4):
        first = jnp.where(place >= ends_ref[k], ends_ref[k], first)
    column = lax.broadcasted_iota(jnp.int32, (rows, seen), 1)
    return jnp.where((column >= first) & (column <= place), scores, f32(-1e30))


def attend(qkv, ends, scale):
    seq_len, cols = qkv.shape
    heads = cols // (3 * HEAD_SIZE)
    tile = min(256, seq_len // 4)

    def kernel(ends_ref, q_ref, k_ref, v_ref, o_ref, lse_ref):
        for begin in range(0, seq_len, tile):
            seen = begin + tile
            scores = scores_of(q_ref[begin:seen, :], k_ref[:seen, :], begin, ends_ref, scale)
            largest = jnp.max(scores, axis=-1, keepdims=True)
            expo = jnp.exp(scores - largest)
            totals = jnp.sum(expo, axis=-1, keepdims=True)
            probs = (expo / totals).astype(bf16)
            o_ref[begin:seen, :] = jnp.dot(
                probs, v_ref[:seen, :], preferred_element_type=f32
            ).astype(bf16)
            lse_ref[begin:seen, :] = jnp.broadcast_to(
                largest + jnp.log(totals), (tile, HEAD_SIZE)
            )

    def spec(kind):
        return pl.BlockSpec((seq_len, HEAD_SIZE), lambda h, e: (0, kind * heads + h))

    return pl.pallas_call(
        kernel,
        grid_spec=pltpu.PrefetchScalarGridSpec(
            num_scalar_prefetch=1,
            grid=(heads,),
            in_specs=[spec(0), spec(1), spec(2)],
            out_specs=[spec(0), spec(0)],
        ),
        out_shape=[
            jax.ShapeDtypeStruct((seq_len, heads * HEAD_SIZE), bf16),
            jax.ShapeDtypeStruct((seq_len, heads * HEAD_SIZE), f32),
        ],
        compiler_params=pltpu.CompilerParams(vmem_limit_bytes=24 * 2**20),
        cost_estimate=cost(6),
    )(ends, qkv, qkv, qkv)


def attend_back(qkv, lse, branch, weight, ends, scale):
    seq_len, cols = qkv.shape
    heads = cols // (3 * HEAD_SIZE)
    own = heads * HEAD_SIZE
    width = weight.shape[0]
    rows = seq_len // len(REL)
    tile = min(256, seq_len // 4)
    pieces, starts = row_pieces(branch, rows)
    count = len(pieces)

    def kernel(ends_ref, place_ref, *refs):
        q_ref, k_ref, v_ref, lse_ref, w_ref = refs[:5]
        out_ref, dk_ref, dv_ref, da_ref, go_ref = refs[5 + count :]
        h = pl.program_id(0)

        @pl.when(h == 0)
        def _():
            for k, start in enumerate(starts):
                i, inside = start // rows, start % rows
                begin = pl.multiple_of(place_ref[i] * rows + inside, rows // 2)
                da_ref[pl.ds(begin, pieces[k].shape[0]), :] = refs[5 + k][...]
            grad = jnp.dot(da_ref[...], w_ref[...], preferred_element_type=f32).astype(bf16)
            for n in range(heads):
                go_ref[n] = grad[:, n * HEAD_SIZE : (n + 1) * HEAD_SIZE]

        def columns(kind):
            return pl.ds(pl.multiple_of((kind * heads + h) * HEAD_SIZE, HEAD_SIZE), HEAD_SIZE)

        dk_ref[...] = jnp.zeros_like(dk_ref)
        dv_ref[...] = jnp.zeros_like(dv_ref)
        for begin in range(0, seq_len, tile):
            seen = begin + tile
            query = q_ref[begin:seen, :]
            scores = scores_of(query, k_ref[:seen, :], begin, ends_ref, scale)
            probs = jnp.exp(scores - lse_ref[begin:seen, 0:1])
            grad = go_ref[h, begin:seen, :]
            grad_probs = lax.dot_general(
                grad, v_ref[:seen, :], (((1,), (1,)), ((), ())), preferred_element_type=f32
            )
            inner = jnp.sum(probs * grad_probs, axis=-1, keepdims=True)
            grad_scores = (probs * (grad_probs - inner)).astype(bf16)
            out_ref[begin:seen, columns(0)] = (
                jnp.dot(grad_scores, k_ref[:seen, :], preferred_element_type=f32) * scale
            ).astype(bf16)
            over_rows = (((0,), (0,)), ((), ()))
            dk_ref[:seen, :] += lax.dot_general(
                grad_scores, query, over_rows, preferred_element_type=f32
            )
            dv_ref[:seen, :] += lax.dot_general(
                probs.astype(bf16), grad, over_rows, preferred_element_type=f32
            )
        out_ref[:, columns(1)] = (dk_ref[...] * scale).astype(bf16)
        out_ref[:, columns(2)] = dv_ref[...].astype(bf16)

    def spec(kind):
        return pl.BlockSpec((seq_len, HEAD_SIZE), lambda h, e, p: (0, kind * heads + h))

    whole = lambda shape: pl.BlockSpec(shape, lambda h, e, p: (0,) * len(shape))
    return pl.pallas_call(
        kernel,
        grid_spec=pltpu.PrefetchScalarGridSpec(
            num_scalar_prefetch=2,
            grid=(heads,),
            in_specs=[
                spec(0),
                spec(1),
                spec(2),
                spec(0),
                pl.BlockSpec((width, own), lambda h, e, p: (0, cols // own)),
            ]
            + [whole(piece.shape) for piece in pieces],
            out_specs=whole((seq_len, cols)),
            scratch_shapes=[
                pltpu.VMEM((seq_len, HEAD_SIZE), f32),
                pltpu.VMEM((seq_len, HEAD_SIZE), f32),
                pltpu.VMEM((seq_len, width), bf16),
                pltpu.VMEM((heads, seq_len, HEAD_SIZE), bf16),
            ],
        ),
        out_shape=jax.ShapeDtypeStruct((seq_len, cols), bf16),
        compiler_params=pltpu.CompilerParams(vmem_limit_bytes=36 * 2**20),
        cost_estimate=cost(12),
    )(ends, block_places(), qkv, qkv, qkv, lse, weight, *pieces)


def local(
    tokens,
    doc_lengths,
    gain_one,
    bias_one,
    w_qkv,
    w_out,
    gain_two,
    bias_two,
    w_up,
    w_down,
    cotangent,
):
    seq_len, width = tokens.shape
    shard = w_qkv.shape[0]
    local_width = w_qkv.shape[2]
    local_heads = local_width // HEAD_SIZE
    rows = seq_len // (NX * NYL)
    x, y = lax.axis_index("x"), lax.axis_index("yl")
    my_rows = (x * NYL + y) * rows
    scale = HEAD_SIZE**-0.5

    wide = 3 * local_width
    small = jnp.stack([gain_one, bias_one, gain_two, bias_two], 0).astype(bf16)
    small = jnp.pad(small.reshape(1, -1), ((0, 15), (0, wide + local_width - 4 * shard)))
    packed = jnp.concatenate([w_qkv.reshape(shard, wide).astype(bf16), w_out.astype(bf16)], 1)
    first_mine = gather_yz(jnp.concatenate([packed, small], 0))
    first_other = lax.ppermute(first_mine, "c", [(0, 1), (1, 0)])
    ends = jnp.cumsum(doc_lengths[0])

    first, mixed, weight, vectors, mean_one, inverse_one = norm_and_qkv(
        tokens, first_mine, first_other, wide
    )
    mlp_weight = jnp.concatenate([w_down.astype(bf16), w_up.astype(bf16)], 1)
    mlp_weight = pair_yh(after(mlp_weight, first_other))
    gain_a, gain_b, bias_b = vectors[0], vectors[2], vectors[3]
    attended, lse = attend(mixed, ends, scale)
    terms = terms_by_block(STEP_ONE, [attended], weight, first=3)
    sum_one = scatter_one(terms)
    later = terms_by_block(LATER_STEPS, [after(attended, *terms[2, 1])], weight, first=3)
    mlp_weight = gather_zc(after(mlp_weight, attended))
    own_tokens = up(lax.dynamic_slice_in_dim(tokens, my_rows, rows, 0))
    own_cot = up(lax.dynamic_slice_in_dim(cotangent, my_rows, rows, 0))
    own_middle = own_tokens + scatter_three(later, scatter_two(later, sum_one))

    own_two, inverse_two = normalize(own_middle)
    second = (own_two * gain_b + bias_b).astype(bf16)
    second_one = gather_one(second)
    second_two = gather_two(second_one)
    grad_hidden, active, second = mlp(
        gather_three(second, second_one, second_two), cotangent, mlp_weight
    )
    hidden = [active, grad_hidden]
    terms = terms_by_block(STEP_ONE, hidden, mlp_weight, relative=True)
    sum_one = scatter_one(terms)
    later = terms_by_block(
        LATER_STEPS, after(hidden, *terms[2, 1]), mlp_weight, relative=True
    )
    sum_two = scatter_two(later, sum_one)
    both = scatter_three(later, sum_two)
    mlp_terms = mlp_gradients(after(second, sum_two[2]), grad_hidden, cotangent, active)
    both = after(both, mlp_terms)
    mlp_grads = scatter_dp(mlp_terms)
    branch_two, grad_second = both[:, :width], both[:, width:]
    output_own = (own_middle + branch_two).astype(bf16)

    grad_middle = own_cot + norm_back(grad_second, own_two, inverse_two, gain_b)
    own_branch = grad_middle.astype(bf16)
    branch_one = gather_one(own_branch)
    branch_two = gather_two(branch_one)
    branch = gather_three(own_branch, branch_one, branch_two)
    output_one = gather_one(after(output_own, branch_two[0]))
    grad_mixed = attend_back(mixed, lse, branch, weight, ends, scale)
    norm = (tokens, mean_one, inverse_one)
    terms, vec_a = terms_by_block(STEP_ONE, [grad_mixed], weight, norm=norm)
    sum_one = scatter_one(terms)
    later, vec_b = terms_by_block(
        LATER_STEPS, [after(grad_mixed, *terms[2, 1])], weight, norm=norm
    )
    sum_two = scatter_two(later, sum_one)
    vec_one = vec_a + vec_b
    vec_two = jnp.stack([jnp.sum(grad_second * own_two, 0), jnp.sum(grad_second, 0)], 0)
    late_vectors = scatter_order(
        jnp.concatenate([vec_one[:2], vec_two, jnp.zeros((4, width), f32)], 0)
    )
    grad_first = scatter_three(later, sum_two)
    late = late_gradients(after(first, *sum_one), grad_mixed, branch, attended, late_vectors)
    late = scatter_dp(late)

    own_one, own_inverse = normalize(own_tokens)
    grad_tokens = (grad_middle + norm_back(grad_first, own_one, own_inverse, gain_a)).astype(bf16)
    output = gather_three(output_own, output_one, gather_two(output_one))
    output = assemble(output, width, bf16, 0)
    grad_one = gather_one(grad_tokens)
    input_grad = gather_three(grad_tokens, grad_one, gather_two(grad_one))
    input_grad = assemble(input_grad, width, f32, 0)
    sums = sum_mp(late[:, wide + local_width : wide + local_width + 4].T)
    return (
        output,
        input_grad,
        sums[0],
        sums[1],
        late[:, :wide].reshape(shard, 3, local_width),
        late[:, wide : wide + local_width],
        sums[2],
        sums[3],
        mlp_grads[:, : w_up.shape[1]],
        mlp_grads[:, w_up.shape[1] :],
    )


def solution(mesh):
    fine = Mesh(mesh.devices.reshape(NYH, NZ, NC, NX, NYL), ("yh", "z", "c", "x", "yl"))
    return jax.shard_map(
        local,
        mesh=fine,
        in_specs=(
            P(DP, None),
            P(DP, None),
            P(DP),
            P(DP),
            P(DP, None, MP),
            P(DP, MP),
            P(DP),
            P(DP),
            P(DP, MP),
            P(DP, MP),
            P(DP, None),
        ),
        out_specs=(
            P(DP, None),
            P(DP, None),
            P(DP),
            P(DP),
            P(DP, None, MP),
            P(DP, MP),
            P(DP),
            P(DP),
            P(DP, MP),
            P(DP, MP),
        ),
        check_vma=False,
    )
```

```python
import jax
import jax.numpy as jnp
from jax import lax
from jax.experimental import pallas as pl
from jax.experimental.pallas import tpu as pltpu
from jax.sharding import Mesh, PartitionSpec as P

HEAD_SIZE = 128
eps = 1e-05
bf16 = jnp.bfloat16
f32 = jnp.float32

MLP_TILE, MLP_VMEM = 256, 44
SMALL = pl.CostEstimate(flops=1, bytes_accessed=1, transcendentals=0)


def cost(micros):
    return pl.CostEstimate(
        flops=int(micros * 1.1e9), bytes_accessed=int(micros * 3.0e6), transcendentals=0
    )


NX, NYL, NZ, NYH, NC = 4, 2, 4, 2, 2
MP = ("x", "yl")
DP = ("yh", "z", "c")
CMP = ("c", "x", "yl")


def up(values):
    return values.astype(f32)


def normalize(values):
    center = values - jnp.mean(values, axis=-1, keepdims=True)
    inverse_std = lax.rsqrt(jnp.mean(center * center, axis=-1, keepdims=True) + eps)
    return (center * inverse_std, inverse_std)


def norm_back(grad_norm, normed, inverse_std, gain):
    scaled = grad_norm * gain
    return inverse_std * (
        scaled
        - jnp.mean(scaled, axis=-1, keepdims=True)
        - normed * jnp.mean(scaled * normed, axis=-1, keepdims=True)
    )


def to_xp(x, y):
    return (x + 1, y)


def to_xm(x, y):
    return (x - 1, y)


def to_y(x, y):
    return (x, y + 1)


def send(values, zero, one):
    pairs = []
    for c in range(NC):
        for x in range(NX):
            for y in range(NYL):
                tx, ty = (zero, one)[c](x, y)
                pairs.append(((c * NX + x) * NYL + y, (c * NX + tx % NX) * NYL + ty % NYL))
    return lax.ppermute(values, CMP, pairs)


def halves(values):
    middle = values.shape[0] // 2
    return values[:middle], values[middle:]


def gather_one(own):
    return send(own, to_xp, to_xp), send(own, to_xm, to_xm), send(own, to_y, to_y)


def columnwise(body, ins, out_rows):
    width = ins[0].shape[1]
    tile = min(1024, width)

    def kernel(core_ref, *refs):
        outs = body(core_ref[0], [ref[...] for ref in refs[: len(ins)]])
        for ref, out in zip(refs[len(ins) :], outs):
            ref[...] = out.astype(bf16)

    return pl.pallas_call(
        kernel,
        grid_spec=pltpu.PrefetchScalarGridSpec(
            num_scalar_prefetch=1,
            grid=(width // tile,),
            in_specs=[pl.BlockSpec((v.shape[0], tile), lambda j, c: (0, j)) for v in ins],
            out_specs=[pl.BlockSpec((rows, tile), lambda j, c: (0, j)) for rows in out_rows],
        ),
        out_shape=[jax.ShapeDtypeStruct((rows, width), bf16) for rows in out_rows],
        compiler_params=pltpu.CompilerParams(vmem_limit_bytes=16 * 2**20),
        cost_estimate=SMALL,
    )(lax.axis_index("c").astype(jnp.int32).reshape(1), *ins)


def gather_two(one):
    p1, p2, q = one
    rows = q.shape[0]

    def body(core, values):
        p1, p2, q = values
        return (
            halves(p1)[0],
            halves(p2)[1],
            jnp.where(core == 0, p1, q),
            jnp.where(core == 0, p2, q),
        )

    o1, o2, r1, r2 = columnwise(body, one, [rows // 2, rows // 2, rows, rows])
    return (
        send(o1, to_xp, to_xp),
        send(o2, to_xm, to_xm),
        send(r1, to_y, to_xp),
        send(r2, to_y, to_xm),
    )


def gather_three(own, one, two):
    (p1, p2, q), (o1, o2, r1, r2) = one, two
    half = o1.shape[0]

    def body(core, values):
        o1, o2, r1, r2 = values
        return (
            jnp.where(core == 0, o1, halves(r1)[0]),
            jnp.where(core == 0, o2, halves(r2)[1]),
        )

    s1, s2 = columnwise(body, two, [half, half])
    s1 = send(s1, to_y, to_xp)
    s2 = send(s2, to_y, to_xm)
    return {
        (0, 0): (own,),
        (1, 0): (p2,),
        (2, 0): (o1, o2),
        (3, 0): (p1,),
        (0, 1): (q,),
        (1, 1): (r2,),
        (2, 1): (s1, s2),
        (3, 1): (r1,),
    }


STEP_ONE = [(2, 1)]
LATER_STEPS = [(1, 1), (3, 1), (2, 0), (1, 0), (3, 0), (0, 1), (0, 0)]


def core_factors(core):
    zero = jnp.where(core == 0, 1.0, 0.0).astype(f32)
    return zero, 1.0 - zero


def scatter_one(blocks):
    h1, h2 = blocks[2, 1]
    return send(h1, to_y, to_xp), send(h2, to_y, to_xm)


def scatter_two(blocks, one):
    rows = blocks[2, 0].shape[0]

    def body(core, values):
        zero, single = core_factors(core)
        b1, b3, b2, s1, s2 = (up(v) for v in values)
        first, second = halves(b1)
        third, fourth = halves(b3)
        g1, g2 = halves(b2)
        return (
            jnp.concatenate([first + single * s1, second], 0),
            jnp.concatenate([third, fourth + single * s2], 0),
            g1 + zero * s1,
            g2 + zero * s2,
        )

    p, q, r1, r2 = columnwise(
        body,
        [blocks[1, 1], blocks[3, 1], blocks[2, 0], *one],
        [rows, rows, rows // 2, rows // 2],
    )
    return (
        send(p, to_y, to_xp),
        send(q, to_y, to_xm),
        send(r1, to_xp, to_xp),
        send(r2, to_xm, to_xm),
    )


def scatter_three(blocks, two):
    rows = blocks[0, 0].shape[0]

    def body(core, values):
        zero, single = core_factors(core)
        b1, b3, b0, p, q, r1, r2 = (up(v) for v in values)
        first, second = halves(b1 + zero * p)
        third, fourth = halves(b3 + zero * q)
        return (
            jnp.concatenate([first + r1, second], 0),
            jnp.concatenate([third, fourth + r2], 0),
            b0 + single * (p + q),
        )

    t1, t2, u = columnwise(
        body, [blocks[1, 0], blocks[3, 0], blocks[0, 1], *two], [rows, rows, rows]
    )
    t1 = send(t1, to_xp, to_xp)
    t2 = send(t2, to_xm, to_xm)
    u = send(u, to_y, to_y)
    return [blocks[0, 0], t1, t2, u]


REL = [(dx, dy) for dy in range(NYL) for dx in range(NX)]
ORDER = [(0, 0), (1, 0), (3, 0), (0, 1), (2, 0), (1, 1), (3, 1), (2, 1)]


def block_index(dx, dy):
    x, y = lax.axis_index("x"), lax.axis_index("yl")
    return ((x + dx) % NX) * NYL + (y + dy) % NYL


def bounce(pieces, starts, rows, width, dtype, first_column):
    count = len(pieces)

    def kernel(*refs):
        place_ref, in_refs, out_ref = refs[0], refs[1 : count + 1], refs[count + 1]
        got = refs[count + 2 : 2 * count + 2]
        cast = refs[2 * count + 2 : -2]
        in_sem, out_sem = refs[-2:]
        loads = [
            pltpu.make_async_copy(
                in_refs[k].at[:, pl.ds(first_column, width)], got[k], in_sem.at[k]
            )
            for k in range(count)
        ]
        for load in loads:
            load.start()
        stores = []
        for k in range(count):
            loads[k].wait()
            source = got[k]
            if cast:
                cast[k][...] = got[k][...].astype(dtype)
                source = cast[k]
            begin = pl.multiple_of(place_ref[k], min(16, pieces[k].shape[0]))
            store = pltpu.make_async_copy(
                source, out_ref.at[pl.ds(begin, pieces[k].shape[0])], out_sem.at[k]
            )
            store.start()
            stores.append(store)
        for store in stores:
            store.wait()

    scratch = [pltpu.VMEM((piece.shape[0], width), bf16) for piece in pieces]
    if dtype != bf16:
        scratch += [pltpu.VMEM((piece.shape[0], width), dtype) for piece in pieces]
    return pl.pallas_call(
        kernel,
        out_shape=jax.ShapeDtypeStruct((rows, width), dtype),
        in_specs=[pl.BlockSpec(memory_space=pltpu.SMEM)]
        + [pl.BlockSpec(memory_space=pl.ANY)] * count,
        out_specs=pl.BlockSpec(memory_space=pl.ANY),
        scratch_shapes=scratch
        + [pltpu.SemaphoreType.DMA((count,)), pltpu.SemaphoreType.DMA((count,))],
        compiler_params=pltpu.CompilerParams(vmem_limit_bytes=20 * 2**20),
        cost_estimate=SMALL,
    )(jnp.stack([jnp.asarray(start, jnp.int32) for start in starts]), *pieces)


def assemble(blocks, width, dtype, first_column):
    rows = blocks[0, 0][0].shape[0]
    pieces, starts = [], []
    for key in ORDER:
        begin = block_index(*key) * rows
        for piece in blocks[key]:
            pieces.append(piece)
            starts.append(begin)
            begin = begin + piece.shape[0]
    return bounce(pieces, starts, rows * len(REL), width, dtype, first_column)


def sum_mp(values):
    copies = jnp.broadcast_to(values[None], (NX * NYL,) + values.shape)
    return jnp.sum(lax.all_to_all(copies, MP, split_axis=0, concat_axis=0, tiled=True), axis=0)


def after(values, *done):
    return lax.optimization_barrier((values,) + done)[0]


def gather_yz(own):
    copies = jnp.broadcast_to(own[None], (NYH * NZ,) + own.shape)
    return lax.all_to_all(copies, ("yh", "z"), split_axis=0, concat_axis=0, tiled=True)


def row_pieces(blocks, rows):
    pieces, starts = [], []
    for i, key in enumerate(REL):
        begin = i * rows
        for piece in blocks[key]:
            pieces.append(piece)
            starts.append(begin)
            begin += piece.shape[0]
    return pieces, starts


def block_places():
    return jnp.stack([block_index(*key) for key in REL]).astype(jnp.int32)


def terms_by_block(keys, parts_of, weight, first=0, relative=False, norm=None):
    seq_len, depth = parts_of[0].shape
    parts, blocks = len(parts_of), len(keys)
    scattered = weight.ndim == 3
    width = weight.shape[0] * weight.shape[1] if scattered else weight.shape[0]
    rows = seq_len // len(REL)
    tile = min(512, width // 4)
    steps = width // tile
    outs = []
    for k, key in enumerate(keys):
        if key == (2, 1):
            outs += [(k, 0, rows // 2), (k, rows // 2, rows // 2)]
        else:
            outs.append((k, 0, rows))

    def kernel(place_ref, *refs):
        lhs_refs = [refs[n * blocks : (n + 1) * blocks] for n in range(parts)]
        w_ref, refs = refs[parts * blocks], refs[parts * blocks + 1 :]
        if norm is not None:
            x_refs, mean_refs, inverse_refs = (
                refs[n * blocks : (n + 1) * blocks] for n in range(3)
            )
            refs = refs[3 * blocks :]
        out_refs, refs = refs[: len(outs)], refs[len(outs) :]
        for part in range(parts):

            @pl.when(pl.program_id(0) // steps == part)
            def _():
                lhs = jnp.concatenate([ref[...] for ref in lhs_refs[part]], 0)
                total = lax.dot_general(
                    lhs,
                    w_ref[...].reshape(tile, depth),
                    (((1,), (1,)), ((), ())),
                    preferred_element_type=f32,
                )
                for out_ref, (k, inside, count) in zip(out_refs, outs):
                    begin = k * rows + inside
                    out_ref[...] = total[begin : begin + count, :].astype(bf16)
                if norm is not None:
                    one = jnp.zeros((1, tile), f32)
                    two = jnp.zeros((1, tile), f32)
                    for k in range(blocks):
                        part_of = total[k * rows : (k + 1) * rows, :]
                        normed = (
                            x_refs[k][...].astype(f32) - mean_refs[k][:, 0:1]
                        ) * inverse_refs[k][:, 0:1]
                        one = one + jnp.sum(part_of * normed, axis=0, keepdims=True)
                        two = two + jnp.sum(part_of, axis=0, keepdims=True)
                    refs[0][0:1, :] = one
                    refs[0][1:2, :] = two

    def rows_spec(k, cols):
        return pl.BlockSpec((rows, cols), lambda j, p: (p[k], 0))

    def tile_spec(k):
        return pl.BlockSpec((rows, tile), lambda j, p: (p[k], j))

    in_specs, operands = [], []
    for lhs in parts_of:
        in_specs += [rows_spec(k, depth) for k in range(blocks)]
        operands += [lhs] * blocks
    if scattered:
        slices, lanes, cols = weight.shape
        half = steps // NYH
        in_specs.append(
            pl.BlockSpec(
                (tile // lanes, 1, lanes, depth),
                lambda j, p: (j % steps % half, j % steps // half, 0, first + j // steps),
            )
        )
        weight = weight.reshape(slices // NYH, NYH, lanes, cols)
    else:
        in_specs.append(pl.BlockSpec((tile, depth), lambda j, p: (j % steps, first + j // steps)))
    operands.append(weight)
    out_specs = [pl.BlockSpec((count, tile), lambda j, p: (0, j)) for _, _, count in outs]
    out_shape = [jax.ShapeDtypeStruct((count, parts * width), bf16) for _, _, count in outs]
    if norm is not None:
        in_specs += [tile_spec(k) for k in range(blocks)]
        in_specs += [rows_spec(k, norm[1].shape[1]) for k in range(blocks)] * 2
        operands += [norm[0]] * blocks + [norm[1]] * blocks + [norm[2]] * blocks
        out_specs.append(pl.BlockSpec((8, tile), lambda j, p: (0, j)))
        out_shape.append(jax.ShapeDtypeStruct((8, width), f32))
    place = jnp.stack(
        [jnp.int32(REL.index(key)) if relative else block_index(*key) for key in keys]
    ).astype(jnp.int32)
    got = pl.pallas_call(
        kernel,
        grid_spec=pltpu.PrefetchScalarGridSpec(
            num_scalar_prefetch=1,
            grid=(parts * steps,),
            in_specs=in_specs,
            out_specs=out_specs,
        ),
        out_shape=out_shape,
        compiler_params=pltpu.CompilerParams(vmem_limit_bytes=28 * 2**20),
        cost_estimate=cost(1 + blocks),
    )(place, *operands)
    found = {}
    for out, (k, inside, count) in zip(got, outs):
        if keys[k] == (2, 1):
            found.setdefault((2, 1), []).append(out)
        else:
            found[keys[k]] = out
    if norm is not None:
        return found, got[-1]
    return found


SCATTER = [
    (n, (n % (NZ * NC)) * NYH + n // (NZ * NC)) for n in range(NYH * NZ * NC)
]


def permuted(values):
    part = values.shape[1] // len(SCATTER)
    order = sorted(SCATTER, key=lambda pair: pair[1])
    return jnp.concatenate([values[:, n * part : (n + 1) * part] for n, _ in order], 1)


def relative_rows(values):
    seq_len, width = values.shape
    rows = seq_len // len(REL)

    def kernel(place_ref, in_ref, out_ref):
        out_ref[...] = permuted(in_ref[...])

    return pl.pallas_call(
        kernel,
        grid_spec=pltpu.PrefetchScalarGridSpec(
            num_scalar_prefetch=1,
            grid=(len(REL),),
            in_specs=[pl.BlockSpec((rows, width), lambda i, p: (p[i], 0))],
            out_specs=pl.BlockSpec((rows, width), lambda i, p: (i, 0)),
        ),
        out_shape=jax.ShapeDtypeStruct((seq_len, width), values.dtype),
        compiler_params=pltpu.CompilerParams(vmem_limit_bytes=16 * 2**20),
        cost_estimate=cost(4),
    )(block_places(), values)


def mlp(second, cotangent, weight):
    seq_len, width = cotangent.shape
    rows = seq_len // len(REL)
    units = weight.shape[2] // 2
    weight = weight.reshape(width, 2 * units)
    tile = min(MLP_TILE, units // 2)
    steps = units // tile
    root, cubic = (2.0 / jnp.pi) ** 0.5, 0.044715
    pieces, starts = row_pieces(second, rows)
    count = len(pieces)

    def kernel(*refs):
        cot_ref, down_ref, up_ref, du_ref, z_ref, h_ref = refs[count:]

        @pl.when(pl.program_id(0) == 0)
        def _():
            for k, start in enumerate(starts):
                h_ref[start : start + pieces[k].shape[0], :] = refs[k][...]

        u = jnp.dot(h_ref[...], up_ref[...], preferred_element_type=f32)
        dz = jnp.dot(cot_ref[...], down_ref[...], preferred_element_type=f32)
        square = u * u
        t = jnp.tanh(root * (u + cubic * (square * u)))
        half = 0.5 * (1.0 + t)
        z_ref[...] = (u * half).astype(bf16)
        slope = half + (0.5 * root) * u * (1.0 - t * t) * (1.0 + (3.0 * cubic) * square)
        du_ref[...] = (dz * slope).astype(bf16)

    whole = lambda shape: pl.BlockSpec(shape, lambda j: (0,) * len(shape))
    return pl.pallas_call(
        kernel,
        grid=(steps,),
        in_specs=[whole(piece.shape) for piece in pieces]
        + [
            whole(cotangent.shape),
            pl.BlockSpec((width, tile), lambda j: (0, j)),
            pl.BlockSpec((width, tile), lambda j: (0, steps + j)),
        ],
        out_specs=[
            pl.BlockSpec((seq_len, tile), lambda j: (0, j)),
            pl.BlockSpec((seq_len, tile), lambda j: (0, j)),
            whole((seq_len, width)),
        ],
        out_shape=[
            jax.ShapeDtypeStruct((seq_len, units), bf16),
            jax.ShapeDtypeStruct((seq_len, units), bf16),
            jax.ShapeDtypeStruct((seq_len, width), bf16),
        ],
        compiler_params=pltpu.CompilerParams(vmem_limit_bytes=MLP_VMEM * 2**20),
        cost_estimate=cost(16),
    )(*pieces, cotangent, weight, weight)


def mlp_gradients(second, grad_hidden, cotangent, active):
    seq_len, width = second.shape
    cols = active.shape[1]
    tile = min(512, width // 2)

    def kernel(h_ref, du_ref, cot_ref, z_ref, out_ref):
        over = (((0,), (0,)), ((), ()))
        out_ref[:, :cols] = lax.dot_general(
            h_ref[...], du_ref[...], over, preferred_element_type=f32
        ).astype(bf16)
        out_ref[:, cols:] = lax.dot_general(
            cot_ref[...], z_ref[...], over, preferred_element_type=f32
        ).astype(bf16)

    lhs = pl.BlockSpec((seq_len, tile), lambda i: (0, i))
    whole = pl.BlockSpec((seq_len, cols), lambda i: (0, 0))
    return pl.pallas_call(
        kernel,
        grid=(width // tile,),
        in_specs=[lhs, whole, lhs, whole],
        out_specs=pl.BlockSpec((tile, 2 * cols), lambda i: (i, 0)),
        out_shape=jax.ShapeDtypeStruct((width, 2 * cols), bf16),
        compiler_params=pltpu.CompilerParams(vmem_limit_bytes=28 * 2**20),
        cost_estimate=cost(11),
    )(second, grad_hidden, cotangent, active)


def late_gradients(first, grad_mixed, branch, attended, vectors):
    seq_len, width = first.shape
    rows = seq_len // len(REL)
    wide, narrow = grad_mixed.shape[1], attended.shape[1]
    slices = NZ * NC
    part = width // (slices * NYH)
    group = 2
    tile = group * NYH * part
    lanes = 128
    pieces, starts = row_pieces(branch, rows)
    count = len(pieces)

    def kernel(place_ref, *refs):
        h_ref, mixed_ref, o_ref, vec_ref = refs[:4]
        da_refs = refs[4 : 4 + NYH * count]
        out_ref, lhs_ref, rhs_ref = refs[4 + NYH * count :]

        @pl.when(pl.program_id(0) == 0)
        def _():
            for i in range(len(REL)):
                begin = pl.multiple_of(place_ref[i] * rows, rows)
                rhs_ref[i * rows : (i + 1) * rows, :] = o_ref[pl.ds(begin, rows), :]

        for k, start in enumerate(starts):
            stop = start + pieces[k].shape[0]
            for n in range(NYH):
                for g in range(group):
                    place = (g * NYH + n) * part
                    lhs_ref[start:stop, place : place + part] = da_refs[n * count + k][
                        :, g * part : (g + 1) * part
                    ]
        over = (((0,), (0,)), ((), ()))
        out_ref[:, :wide] = lax.dot_general(
            h_ref[...], mixed_ref[...], over, preferred_element_type=f32
        ).astype(bf16)
        out_ref[:, wide : wide + narrow] = lax.dot_general(
            lhs_ref[...], rhs_ref[...], over, preferred_element_type=f32
        ).astype(bf16)
        padded = jnp.concatenate([vec_ref[...], jnp.zeros((lanes - 8, tile), f32)], 0)
        out_ref[:, wide + narrow :] = padded.T.astype(bf16)

    whole = lambda shape: pl.BlockSpec(shape, lambda i, p: (0,) * len(shape))
    steps = slices // group
    near = [pl.BlockSpec((v.shape[0], group * part), lambda i, p: (0, i)) for v in pieces]
    far = [pl.BlockSpec((v.shape[0], group * part), lambda i, p: (0, steps + i)) for v in pieces]
    return pl.pallas_call(
        kernel,
        grid_spec=pltpu.PrefetchScalarGridSpec(
            num_scalar_prefetch=1,
            grid=(steps,),
            in_specs=[
                pl.BlockSpec((seq_len, tile), lambda i, p: (0, i)),
                whole(grad_mixed.shape),
                whole(attended.shape),
                pl.BlockSpec((8, tile), lambda i, p: (0, i)),
            ]
            + near
            + far,
            out_specs=pl.BlockSpec((tile, wide + narrow + lanes), lambda i, p: (i, 0)),
            scratch_shapes=[
                pltpu.VMEM((seq_len, tile), bf16),
                pltpu.VMEM((seq_len, narrow), bf16),
            ],
        ),
        out_shape=jax.ShapeDtypeStruct((width, wide + narrow + lanes), bf16),
        compiler_params=pltpu.CompilerParams(vmem_limit_bytes=24 * 2**20),
        cost_estimate=cost(11),
    )(block_places(), first, grad_mixed, attended, vectors, *pieces, *pieces)


def scatter_order(values):
    shape = values.shape
    values = values.reshape(shape[:-1] + (NYH, NZ * NC, -1))
    return jnp.swapaxes(values, -3, -2).reshape(shape)


def pair_yh(own):
    other = lax.ppermute(own, "yh", [(0, 1), (1, 0)])
    first = lax.axis_index("yh") == 0
    return jnp.stack([jnp.where(first, own, other), jnp.where(first, other, own)], 0)


def gather_zc(pair):
    return lax.all_gather(pair, ("z", "c"), axis=0, tiled=True)


def scatter_dp(values):
    values = lax.psum_scatter(values, ("z", "c"), scatter_dimension=0, tiled=True)
    yh = lax.axis_index("yh")
    rows = values.shape[0] // NYH
    home = lax.dynamic_slice_in_dim(values, yh * rows, rows, 0)
    away = lax.dynamic_slice_in_dim(values, (1 - yh) * rows, rows, 0)
    return up(home) + up(lax.ppermute(away, "yh", [(0, 1), (1, 0)]))


def on_own_rows(body, terms, row_arrays, own_arrays, gains, outs):
    rows = terms[0].shape[0]
    ins = terms + row_arrays + own_arrays + gains

    def kernel(place_ref, *refs):
        values = [ref[...] for ref in refs[: len(ins)]]
        total = up(values[0])
        for value in values[1 : len(terms)]:
            total = total + up(value)
        results = body(total, *values[len(terms) :])
        for ref, result in zip(refs[len(ins) :], results):
            ref[...] = result.astype(ref.dtype)

    whole = lambda shape: pl.BlockSpec(shape, lambda i, p: (0, 0))
    return pl.pallas_call(
        kernel,
        grid_spec=pltpu.PrefetchScalarGridSpec(
            num_scalar_prefetch=1,
            grid=(1,),
            in_specs=[whole(v.shape) for v in terms]
            + [pl.BlockSpec((rows, v.shape[1]), lambda i, p: (p[0], 0)) for v in row_arrays]
            + [whole(v.shape) for v in own_arrays + gains],
            out_specs=[whole(shape) for shape, _ in outs],
        ),
        out_shape=[jax.ShapeDtypeStruct(shape, dtype) for shape, dtype in outs],
        compiler_params=pltpu.CompilerParams(vmem_limit_bytes=32 * 2**20),
        cost_estimate=SMALL,
    )(block_index(0, 0).astype(jnp.int32).reshape(1), *ins)


def norm_and_qkv(tokens, mine, other, cols):
    seq_len, width = tokens.shape
    slices, packed_rows, all_cols = mine.shape
    shard = packed_rows - 16
    tile = min(256, seq_len // 4)

    def kernel(
        place_ref, x_ref, mine_ref, other_ref, h_ref, qkv_ref, w_ref, vec_ref, mean_ref, inverse_ref
    ):
        core = place_ref[0]

        @pl.when(pl.program_id(0) == 0)
        def _():
            for ref, parity in ((mine_ref, core), (other_ref, 1 - core)):
                for s in range(slices):
                    begin = pl.multiple_of((NC * s + parity) * shard, shard)
                    w_ref[pl.ds(begin, shard), :] = ref[s, :shard, :]
                    row = ref[s, shard:, :].astype(f32)
                    for k in range(4):
                        vec_ref[k : k + 1, pl.ds(begin, shard)] = row[
                            0:1, k * shard : (k + 1) * shard
                        ]

        x = x_ref[...].astype(f32)
        mean = jnp.mean(x, axis=-1, keepdims=True)
        center = x - mean
        inverse = lax.rsqrt(jnp.mean(center * center, axis=-1, keepdims=True) + eps)
        mean_ref[...] = jnp.broadcast_to(mean, mean_ref.shape)
        inverse_ref[...] = jnp.broadcast_to(inverse, inverse_ref.shape)
        h = (center * inverse * vec_ref[0:1, :] + vec_ref[1:2, :]).astype(bf16)
        for n in range(NYH * NZ * NC):
            place = (n % (NZ * NC)) * NYH + n // (NZ * NC)
            h_ref[:, place * shard : (place + 1) * shard] = h[:, n * shard : (n + 1) * shard]
        qkv_ref[...] = jnp.dot(h, w_ref[:, :cols], preferred_element_type=f32).astype(bf16)

    whole = lambda shape: pl.BlockSpec(shape, lambda i, p: (0,) * len(shape))
    place = lax.axis_index("c").astype(jnp.int32).reshape(1)
    return pl.pallas_call(
        kernel,
        grid_spec=pltpu.PrefetchScalarGridSpec(
            num_scalar_prefetch=1,
            grid=(seq_len // tile,),
            in_specs=[
                pl.BlockSpec((tile, width), lambda i, p: (i, 0)),
                whole(mine.shape),
                whole(other.shape),
            ],
            out_specs=[
                pl.BlockSpec((tile, width), lambda i, p: (i, 0)),
                pl.BlockSpec((tile, cols), lambda i, p: (i, 0)),
                whole((width, all_cols)),
                whole((8, width)),
                pl.BlockSpec((tile, 128), lambda i, p: (i, 0)),
                pl.BlockSpec((tile, 128), lambda i, p: (i, 0)),
            ],
        ),
        out_shape=[
            jax.ShapeDtypeStruct((seq_len, width), bf16),
            jax.ShapeDtypeStruct((seq_len, cols), bf16),
            jax.ShapeDtypeStruct((width, all_cols), bf16),
            jax.ShapeDtypeStruct((8, width), f32),
            jax.ShapeDtypeStruct((seq_len, 128), f32),
            jax.ShapeDtypeStruct((seq_len, 128), f32),
        ],
        compiler_params=pltpu.CompilerParams(vmem_limit_bytes=36 * 2**20),
        cost_estimate=cost(9),
    )(place, tokens, mine, other)


def scores_of(query, keys, begin, ends_ref, scale):
    rows, seen = query.shape[0], keys.shape[0]
    scores = (
        lax.dot_general(query, keys, (((1,), (1,)), ((), ())), preferred_element_type=f32) * scale
    )
    place = begin + lax.broadcasted_iota(jnp.int32, (rows, 1), 0)
    first = jnp.zeros((rows, 1), jnp.int32)
    for k in range(4):
        first = jnp.where(place >= ends_ref[k], ends_ref[k], first)
    column = lax.broadcasted_iota(jnp.int32, (rows, seen), 1)
    return jnp.where((column >= first) & (column <= place), scores, f32(-1e30))


def attend(qkv, ends, scale):
    seq_len, cols = qkv.shape
    heads = cols // (3 * HEAD_SIZE)
    tile = min(256, seq_len // 4)

    def kernel(ends_ref, q_ref, k_ref, v_ref, o_ref, lse_ref):
        for begin in range(0, seq_len, tile):
            seen = begin + tile
            scores = scores_of(q_ref[begin:seen, :], k_ref[:seen, :], begin, ends_ref, scale)
            largest = jnp.max(scores, axis=-1, keepdims=True)
            expo = jnp.exp(scores - largest)
            totals = jnp.sum(expo, axis=-1, keepdims=True)
            probs = (expo / totals).astype(bf16)
            o_ref[begin:seen, :] = jnp.dot(
                probs, v_ref[:seen, :], preferred_element_type=f32
            ).astype(bf16)
            lse_ref[begin:seen, :] = jnp.broadcast_to(
                largest + jnp.log(totals), (tile, HEAD_SIZE)
            )

    def spec(kind):
        return pl.BlockSpec((seq_len, HEAD_SIZE), lambda h, e: (0, kind * heads + h))

    return pl.pallas_call(
        kernel,
        grid_spec=pltpu.PrefetchScalarGridSpec(
            num_scalar_prefetch=1,
            grid=(heads,),
            in_specs=[spec(0), spec(1), spec(2)],
            out_specs=[spec(0), spec(0)],
        ),
        out_shape=[
            jax.ShapeDtypeStruct((seq_len, heads * HEAD_SIZE), bf16),
            jax.ShapeDtypeStruct((seq_len, heads * HEAD_SIZE), f32),
        ],
        compiler_params=pltpu.CompilerParams(vmem_limit_bytes=24 * 2**20),
        cost_estimate=cost(6),
    )(ends, qkv, qkv, qkv)


def attend_back(qkv, lse, branch, weight, ends, scale):
    seq_len, cols = qkv.shape
    heads = cols // (3 * HEAD_SIZE)
    own = heads * HEAD_SIZE
    width = weight.shape[0]
    rows = seq_len // len(REL)
    tile = min(256, seq_len // 4)
    pieces, starts = row_pieces(branch, rows)
    count = len(pieces)

    def kernel(ends_ref, place_ref, *refs):
        q_ref, k_ref, v_ref, lse_ref, w_ref = refs[:5]
        out_ref, dk_ref, dv_ref, da_ref, go_ref = refs[5 + count :]
        h = pl.program_id(0)

        @pl.when(h == 0)
        def _():
            for k, start in enumerate(starts):
                i, inside = start // rows, start % rows
                begin = pl.multiple_of(place_ref[i] * rows + inside, rows // 2)
                da_ref[pl.ds(begin, pieces[k].shape[0]), :] = refs[5 + k][...]
            grad = jnp.dot(da_ref[...], w_ref[...], preferred_element_type=f32).astype(bf16)
            for n in range(heads):
                go_ref[n] = grad[:, n * HEAD_SIZE : (n + 1) * HEAD_SIZE]

        def columns(kind):
            return pl.ds(pl.multiple_of((kind * heads + h) * HEAD_SIZE, HEAD_SIZE), HEAD_SIZE)

        dk_ref[...] = jnp.zeros_like(dk_ref)
        dv_ref[...] = jnp.zeros_like(dv_ref)
        for begin in range(0, seq_len, tile):
            seen = begin + tile
            query = q_ref[begin:seen, :]
            scores = scores_of(query, k_ref[:seen, :], begin, ends_ref, scale)
            probs = jnp.exp(scores - lse_ref[begin:seen, 0:1])
            grad = go_ref[h, begin:seen, :]
            grad_probs = lax.dot_general(
                grad, v_ref[:seen, :], (((1,), (1,)), ((), ())), preferred_element_type=f32
            )
            inner = jnp.sum(probs * grad_probs, axis=-1, keepdims=True)
            grad_scores = (probs * (grad_probs - inner)).astype(bf16)
            out_ref[begin:seen, columns(0)] = (
                jnp.dot(grad_scores, k_ref[:seen, :], preferred_element_type=f32) * scale
            ).astype(bf16)
            over_rows = (((0,), (0,)), ((), ()))
            dk_ref[:seen, :] += lax.dot_general(
                grad_scores, query, over_rows, preferred_element_type=f32
            )
            dv_ref[:seen, :] += lax.dot_general(
                probs.astype(bf16), grad, over_rows, preferred_element_type=f32
            )
        out_ref[:, columns(1)] = (dk_ref[...] * scale).astype(bf16)
        out_ref[:, columns(2)] = dv_ref[...].astype(bf16)

    def spec(kind):
        return pl.BlockSpec((seq_len, HEAD_SIZE), lambda h, e, p: (0, kind * heads + h))

    whole = lambda shape: pl.BlockSpec(shape, lambda h, e, p: (0,) * len(shape))
    return pl.pallas_call(
        kernel,
        grid_spec=pltpu.PrefetchScalarGridSpec(
            num_scalar_prefetch=2,
            grid=(heads,),
            in_specs=[
                spec(0),
                spec(1),
                spec(2),
                spec(0),
                pl.BlockSpec((width, own), lambda h, e, p: (0, cols // own)),
            ]
            + [whole(piece.shape) for piece in pieces],
            out_specs=whole((seq_len, cols)),
            scratch_shapes=[
                pltpu.VMEM((seq_len, HEAD_SIZE), f32),
                pltpu.VMEM((seq_len, HEAD_SIZE), f32),
                pltpu.VMEM((seq_len, width), bf16),
                pltpu.VMEM((heads, seq_len, HEAD_SIZE), bf16),
            ],
        ),
        out_shape=jax.ShapeDtypeStruct((seq_len, cols), bf16),
        compiler_params=pltpu.CompilerParams(vmem_limit_bytes=36 * 2**20),
        cost_estimate=cost(12),
    )(ends, block_places(), qkv, qkv, qkv, lse, weight, *pieces)


def local(
    tokens,
    doc_lengths,
    gain_one,
    bias_one,
    w_qkv,
    w_out,
    gain_two,
    bias_two,
    w_up,
    w_down,
    cotangent,
):
    seq_len, width = tokens.shape
    shard = w_qkv.shape[0]
    local_width = w_qkv.shape[2]
    local_heads = local_width // HEAD_SIZE
    rows = seq_len // (NX * NYL)
    x, y = lax.axis_index("x"), lax.axis_index("yl")
    scale = HEAD_SIZE**-0.5

    wide = 3 * local_width
    small = jnp.stack([gain_one, bias_one, gain_two, bias_two], 0).astype(bf16)
    small = jnp.pad(small.reshape(1, -1), ((0, 15), (0, wide + local_width - 4 * shard)))
    packed = jnp.concatenate([w_qkv.reshape(shard, wide).astype(bf16), w_out.astype(bf16)], 1)
    first_mine = gather_yz(jnp.concatenate([packed, small], 0))
    first_other = lax.ppermute(first_mine, "c", [(0, 1), (1, 0)])
    cot_order = relative_rows(cotangent)
    ends = jnp.cumsum(doc_lengths[0])

    first, mixed, weight, vectors, mean_one, inverse_one = norm_and_qkv(
        tokens, first_mine, first_other, wide
    )
    mlp_weight = jnp.concatenate([w_down.astype(bf16), w_up.astype(bf16)], 1)
    mlp_weight = pair_yh(after(mlp_weight, first_other))
    gain_a, gain_b, bias_b = vectors[0], vectors[2], vectors[3]
    attended, lse = attend(mixed, ends, scale)
    terms = terms_by_block(STEP_ONE, [attended], weight, first=3)
    sum_one = scatter_one(terms)
    later = terms_by_block(LATER_STEPS, [after(attended, *terms[2, 1])], weight, first=3)
    mlp_weight = gather_zc(after(mlp_weight, attended))
    own_f32, own_bf16 = ((rows, width), f32), ((rows, width), bf16)
    gain_a, gain_b, bias_b = (v.reshape(1, width) for v in (gain_a, gain_b, bias_b))

    def second_norm(branch, x, gain, bias):
        middle = up(x) + branch
        normed, _ = normalize(middle)
        return middle, permuted((normed * gain + bias).astype(bf16))

    own_middle, second = on_own_rows(
        second_norm,
        scatter_three(later, scatter_two(later, sum_one)),
        [tokens],
        [],
        [gain_b, bias_b],
        [own_f32, own_bf16],
    )

    second_one = gather_one(second)
    second_two = gather_two(second_one)
    grad_hidden, active, second = mlp(
        gather_three(second, second_one, second_two), cot_order, mlp_weight
    )
    hidden = [active, grad_hidden]
    terms = terms_by_block(STEP_ONE, hidden, mlp_weight, relative=True)
    sum_one = scatter_one(terms)
    later = terms_by_block(
        LATER_STEPS, after(hidden, *terms[2, 1]), mlp_weight, relative=True
    )
    sum_two = scatter_two(later, sum_one)
    both = scatter_three(later, sum_two)
    mlp_terms = mlp_gradients(after(second, sum_two[2]), grad_hidden, cot_order, active)
    both = after(both, mlp_terms)
    mlp_grads = scatter_dp(mlp_terms)
    grad_up, grad_down = mlp_grads[:, : w_up.shape[1]], mlp_grads[:, w_up.shape[1] :]

    def second_norm_back(both, cot, middle, gain):
        grad = both[:, width:]
        normed, inverse = normalize(middle)
        vector = jnp.concatenate(
            [
                jnp.sum(grad * normed, axis=0, keepdims=True),
                jnp.sum(grad, axis=0, keepdims=True),
                jnp.zeros((6, width), f32),
            ],
            0,
        )
        back = up(cot) + norm_back(grad, normed, inverse, gain)
        return middle + both[:, :width], back, back, vector

    output_own, grad_middle, own_branch, vec_two = on_own_rows(
        second_norm_back,
        both,
        [cotangent],
        [own_middle],
        [gain_b],
        [own_bf16, own_f32, own_bf16, ((8, width), f32)],
    )
    branch_one = gather_one(own_branch)
    branch_two = gather_two(branch_one)
    branch = gather_three(own_branch, branch_one, branch_two)
    output_one = gather_one(after(output_own, branch_two[0]))
    grad_mixed = attend_back(mixed, lse, branch, weight, ends, scale)
    norm = (tokens, mean_one, inverse_one)
    terms, vec_a = terms_by_block(STEP_ONE, [grad_mixed], weight, norm=norm)
    sum_one = scatter_one(terms)
    later, vec_b = terms_by_block(
        LATER_STEPS, [after(grad_mixed, *terms[2, 1])], weight, norm=norm
    )
    sum_two = scatter_two(later, sum_one)
    vec_one = vec_a + vec_b
    late_vectors = scatter_order(
        jnp.concatenate([vec_one[:2], vec_two[:2], jnp.zeros((4, width), f32)], 0)
    )
    grad_first = scatter_three(later, sum_two)
    late = late_gradients(after(first, *sum_one), grad_mixed, branch, attended, late_vectors)
    late = scatter_dp(late)

    def first_norm_back(grad, x, middle, gain):
        normed, inverse = normalize(up(x))
        return [middle + norm_back(grad, normed, inverse, gain)]

    (grad_tokens,) = on_own_rows(
        first_norm_back, grad_first, [tokens], [grad_middle], [gain_a], [own_bf16]
    )
    output = gather_three(output_own, output_one, gather_two(output_one))
    output = assemble(output, width, bf16, 0)
    grad_one = gather_one(grad_tokens)
    input_grad = gather_three(grad_tokens, grad_one, gather_two(grad_one))
    sums = sum_mp(late[:, wide + local_width : wide + local_width + 4].T)
    input_grad, sums = lax.optimization_barrier((input_grad, sums))
    input_grad = assemble(input_grad, width, f32, 0)
    return (
        output,
        input_grad,
        sums[0],
        sums[1],
        late[:, :wide].reshape(shard, 3, local_width),
        late[:, wide : wide + local_width],
        sums[2],
        sums[3],
        grad_up,
        grad_down,
    )


def solution(mesh):
    fine = Mesh(mesh.devices.reshape(NYH, NZ, NC, NX, NYL), ("yh", "z", "c", "x", "yl"))
    return jax.shard_map(
        local,
        mesh=fine,
        in_specs=(
            P(DP, None),
            P(DP, None),
            P(DP),
            P(DP),
            P(DP, None, MP),
            P(DP, MP),
            P(DP),
            P(DP),
            P(DP, MP),
            P(DP, MP),
            P(DP, None),
        ),
        out_specs=(
            P(DP, None),
            P(DP, None),
            P(DP),
            P(DP),
            P(DP, None, MP),
            P(DP, MP),
            P(DP),
            P(DP),
            P(DP, MP),
            P(DP, MP),
        ),
        check_vma=False,
    )
```

```python
import jax
import jax.numpy as jnp
from jax import lax
from jax.experimental import pallas as pl
from jax.experimental.pallas import tpu as pltpu
from jax.sharding import Mesh, PartitionSpec as P

HEAD_SIZE = 128
eps = 1e-05
bf16 = jnp.bfloat16
f32 = jnp.float32

MLP_TILE, MLP_VMEM = 512, 40
SMALL = pl.CostEstimate(flops=1, bytes_accessed=1, transcendentals=0)


def cost(micros):
    return pl.CostEstimate(
        flops=int(micros * 1.1e9), bytes_accessed=int(micros * 3.0e6), transcendentals=0
    )


NX, NYL, NZ, NYH, NC = 4, 2, 4, 2, 2
MP = ("x", "yl")
DP = ("yh", "z", "c")
CMP = ("c", "x", "yl")


def up(values):
    return values.astype(f32)


def normalize(values):
    center = values - jnp.mean(values, axis=-1, keepdims=True)
    inverse_std = lax.rsqrt(jnp.mean(center * center, axis=-1, keepdims=True) + eps)
    return (center * inverse_std, inverse_std)


def norm_back(grad_norm, normed, inverse_std, gain):
    scaled = grad_norm * gain
    return inverse_std * (
        scaled
        - jnp.mean(scaled, axis=-1, keepdims=True)
        - normed * jnp.mean(scaled * normed, axis=-1, keepdims=True)
    )


def to_xp(x, y):
    return (x + 1, y)


def to_xm(x, y):
    return (x - 1, y)


def to_y(x, y):
    return (x, y + 1)


def send(values, zero, one):
    pairs = []
    for c in range(NC):
        for x in range(NX):
            for y in range(NYL):
                tx, ty = (zero, one)[c](x, y)
                pairs.append(((c * NX + x) * NYL + y, (c * NX + tx % NX) * NYL + ty % NYL))
    return lax.ppermute(values, CMP, pairs)


def halves(values):
    middle = values.shape[0] // 2
    return values[:middle], values[middle:]


def gather_one(own):
    return send(own, to_xp, to_xp), send(own, to_xm, to_xm), send(own, to_y, to_y)


def columnwise(body, ins, out_rows):
    width = ins[0].shape[1]
    tile = min(1024, width)

    def kernel(core_ref, *refs):
        outs = body(core_ref[0], [ref[...] for ref in refs[: len(ins)]])
        for ref, out in zip(refs[len(ins) :], outs):
            ref[...] = out.astype(bf16)

    return pl.pallas_call(
        kernel,
        grid_spec=pltpu.PrefetchScalarGridSpec(
            num_scalar_prefetch=1,
            grid=(width // tile,),
            in_specs=[pl.BlockSpec((v.shape[0], tile), lambda j, c: (0, j)) for v in ins],
            out_specs=[pl.BlockSpec((rows, tile), lambda j, c: (0, j)) for rows in out_rows],
        ),
        out_shape=[jax.ShapeDtypeStruct((rows, width), bf16) for rows in out_rows],
        compiler_params=pltpu.CompilerParams(vmem_limit_bytes=16 * 2**20),
        cost_estimate=SMALL,
    )(lax.axis_index("c").astype(jnp.int32).reshape(1), *ins)


def gather_two(one):
    p1, p2, q = one
    rows = q.shape[0]

    def body(core, values):
        p1, p2, q = values
        return (
            halves(p1)[0],
            halves(p2)[1],
            jnp.where(core == 0, p1, q),
            jnp.where(core == 0, p2, q),
        )

    o1, o2, r1, r2 = columnwise(body, one, [rows // 2, rows // 2, rows, rows])
    return (
        send(o1, to_xp, to_xp),
        send(o2, to_xm, to_xm),
        send(r1, to_y, to_xp),
        send(r2, to_y, to_xm),
    )


def gather_three(own, one, two):
    (p1, p2, q), (o1, o2, r1, r2) = one, two
    half = o1.shape[0]

    def body(core, values):
        o1, o2, r1, r2 = values
        return (
            jnp.where(core == 0, o1, halves(r1)[0]),
            jnp.where(core == 0, o2, halves(r2)[1]),
        )

    s1, s2 = columnwise(body, two, [half, half])
    s1 = send(s1, to_y, to_xp)
    s2 = send(s2, to_y, to_xm)
    return {
        (0, 0): (own,),
        (1, 0): (p2,),
        (2, 0): (o1, o2),
        (3, 0): (p1,),
        (0, 1): (q,),
        (1, 1): (r2,),
        (2, 1): (s1, s2),
        (3, 1): (r1,),
    }


STEP_ONE = [(2, 1)]
LATER_STEPS = [(1, 1), (3, 1), (2, 0), (1, 0), (3, 0), (0, 1), (0, 0)]


def core_factors(core):
    zero = jnp.where(core == 0, 1.0, 0.0).astype(f32)
    return zero, 1.0 - zero


def scatter_one(blocks):
    h1, h2 = blocks[2, 1]
    return send(h1, to_y, to_xp), send(h2, to_y, to_xm)


def scatter_two(blocks, one):
    rows = blocks[2, 0].shape[0]

    def body(core, values):
        zero, single = core_factors(core)
        b1, b3, b2, s1, s2 = (up(v) for v in values)
        first, second = halves(b1)
        third, fourth = halves(b3)
        g1, g2 = halves(b2)
        return (
            jnp.concatenate([first + single * s1, second], 0),
            jnp.concatenate([third, fourth + single * s2], 0),
            g1 + zero * s1,
            g2 + zero * s2,
        )

    p, q, r1, r2 = columnwise(
        body,
        [blocks[1, 1], blocks[3, 1], blocks[2, 0], *one],
        [rows, rows, rows // 2, rows // 2],
    )
    return (
        send(p, to_y, to_xp),
        send(q, to_y, to_xm),
        send(r1, to_xp, to_xp),
        send(r2, to_xm, to_xm),
    )


def scatter_three(blocks, two):
    rows = blocks[0, 0].shape[0]

    def body(core, values):
        zero, single = core_factors(core)
        b1, b3, b0, p, q, r1, r2 = (up(v) for v in values)
        first, second = halves(b1 + zero * p)
        third, fourth = halves(b3 + zero * q)
        return (
            jnp.concatenate([first + r1, second], 0),
            jnp.concatenate([third, fourth + r2], 0),
            b0 + single * (p + q),
        )

    t1, t2, u = columnwise(
        body, [blocks[1, 0], blocks[3, 0], blocks[0, 1], *two], [rows, rows, rows]
    )
    t1 = send(t1, to_xp, to_xp)
    t2 = send(t2, to_xm, to_xm)
    u = send(u, to_y, to_y)
    return [blocks[0, 0], t1, t2, u]


REL = [(dx, dy) for dy in range(NYL) for dx in range(NX)]
ORDER = [(0, 0), (1, 0), (3, 0), (0, 1), (2, 0), (1, 1), (3, 1), (2, 1)]


def block_index(dx, dy):
    x, y = lax.axis_index("x"), lax.axis_index("yl")
    return ((x + dx) % NX) * NYL + (y + dy) % NYL


def bounce(pieces, starts, rows, width, dtype, first_column):
    count = len(pieces)

    def kernel(*refs):
        place_ref, in_refs, out_ref = refs[0], refs[1 : count + 1], refs[count + 1]
        got = refs[count + 2 : 2 * count + 2]
        cast = refs[2 * count + 2 : -2]
        in_sem, out_sem = refs[-2:]
        loads = [
            pltpu.make_async_copy(
                in_refs[k].at[:, pl.ds(first_column, width)], got[k], in_sem.at[k]
            )
            for k in range(count)
        ]
        for load in loads:
            load.start()
        stores = []
        for k in range(count):
            loads[k].wait()
            source = got[k]
            if cast:
                cast[k][...] = got[k][...].astype(dtype)
                source = cast[k]
            begin = pl.multiple_of(place_ref[k], min(16, pieces[k].shape[0]))
            store = pltpu.make_async_copy(
                source, out_ref.at[pl.ds(begin, pieces[k].shape[0])], out_sem.at[k]
            )
            store.start()
            stores.append(store)
        for store in stores:
            store.wait()

    scratch = [pltpu.VMEM((piece.shape[0], width), bf16) for piece in pieces]
    if dtype != bf16:
        scratch += [pltpu.VMEM((piece.shape[0], width), dtype) for piece in pieces]
    return pl.pallas_call(
        kernel,
        out_shape=jax.ShapeDtypeStruct((rows, width), dtype),
        in_specs=[pl.BlockSpec(memory_space=pltpu.SMEM)]
        + [pl.BlockSpec(memory_space=pl.ANY)] * count,
        out_specs=pl.BlockSpec(memory_space=pl.ANY),
        scratch_shapes=scratch
        + [pltpu.SemaphoreType.DMA((count,)), pltpu.SemaphoreType.DMA((count,))],
        compiler_params=pltpu.CompilerParams(vmem_limit_bytes=20 * 2**20),
        cost_estimate=SMALL,
    )(jnp.stack([jnp.asarray(start, jnp.int32) for start in starts]), *pieces)


def assemble(blocks, width, dtype, first_column):
    rows = blocks[0, 0][0].shape[0]
    pieces, starts = [], []
    for key in ORDER:
        begin = block_index(*key) * rows
        for piece in blocks[key]:
            pieces.append(piece)
            starts.append(begin)
            begin = begin + piece.shape[0]
    return bounce(pieces, starts, rows * len(REL), width, dtype, first_column)


def sum_mp(values):
    copies = jnp.broadcast_to(values[None], (NX * NYL,) + values.shape)
    return jnp.sum(lax.all_to_all(copies, MP, split_axis=0, concat_axis=0, tiled=True), axis=0)


def after(values, *done):
    return lax.optimization_barrier((values,) + done)[0]


def gather_yz(own):
    copies = jnp.broadcast_to(own[None], (NYH * NZ,) + own.shape)
    return lax.all_to_all(copies, ("yh", "z"), split_axis=0, concat_axis=0, tiled=True)


def row_pieces(blocks, rows):
    pieces, starts = [], []
    for i, key in enumerate(REL):
        begin = i * rows
        for piece in blocks[key]:
            pieces.append(piece)
            starts.append(begin)
            begin += piece.shape[0]
    return pieces, starts


def block_places():
    return jnp.stack([block_index(*key) for key in REL]).astype(jnp.int32)


def terms_by_block(keys, parts_of, weight, first=0, relative=False, norm=None):
    seq_len, depth = parts_of[0].shape
    parts, blocks = len(parts_of), len(keys)
    scattered = weight.ndim == 3
    width = weight.shape[0] * weight.shape[1] if scattered else weight.shape[0]
    rows = seq_len // len(REL)
    tile = min(512, width // 4)
    steps = width // tile
    outs = []
    for k, key in enumerate(keys):
        if key == (2, 1):
            outs += [(k, 0, rows // 2), (k, rows // 2, rows // 2)]
        else:
            outs.append((k, 0, rows))

    def kernel(place_ref, *refs):
        lhs_refs = [refs[n * blocks : (n + 1) * blocks] for n in range(parts)]
        w_ref, refs = refs[parts * blocks], refs[parts * blocks + 1 :]
        if norm is not None:
            x_refs, mean_refs, inverse_refs = (
                refs[n * blocks : (n + 1) * blocks] for n in range(3)
            )
            refs = refs[3 * blocks :]
        out_refs, refs = refs[: len(outs)], refs[len(outs) :]
        for part in range(parts):

            @pl.when(pl.program_id(0) // steps == part)
            def _():
                lhs = jnp.concatenate([ref[...] for ref in lhs_refs[part]], 0)
                total = lax.dot_general(
                    lhs,
                    w_ref[...].reshape(tile, depth),
                    (((1,), (1,)), ((), ())),
                    preferred_element_type=f32,
                )
                for out_ref, (k, inside, count) in zip(out_refs, outs):
                    begin = k * rows + inside
                    out_ref[...] = total[begin : begin + count, :].astype(bf16)
                if norm is not None:
                    one = jnp.zeros((1, tile), f32)
                    two = jnp.zeros((1, tile), f32)
                    for k in range(blocks):
                        part_of = total[k * rows : (k + 1) * rows, :]
                        normed = (
                            x_refs[k][...].astype(f32) - mean_refs[k][:, 0:1]
                        ) * inverse_refs[k][:, 0:1]
                        one = one + jnp.sum(part_of * normed, axis=0, keepdims=True)
                        two = two + jnp.sum(part_of, axis=0, keepdims=True)
                    refs[0][0:1, :] = one
                    refs[0][1:2, :] = two

    def rows_spec(k, cols):
        return pl.BlockSpec((rows, cols), lambda j, p: (p[k], 0))

    def tile_spec(k):
        return pl.BlockSpec((rows, tile), lambda j, p: (p[k], j))

    in_specs, operands = [], []
    for lhs in parts_of:
        in_specs += [rows_spec(k, depth) for k in range(blocks)]
        operands += [lhs] * blocks
    if scattered:
        slices, lanes, cols = weight.shape
        half = steps // NYH
        in_specs.append(
            pl.BlockSpec(
                (tile // lanes, 1, lanes, depth),
                lambda j, p: (j % steps % half, j % steps // half, 0, first + j // steps),
            )
        )
        weight = weight.reshape(slices // NYH, NYH, lanes, cols)
    else:
        in_specs.append(pl.BlockSpec((tile, depth), lambda j, p: (j % steps, first + j // steps)))
    operands.append(weight)
    out_specs = [pl.BlockSpec((count, tile), lambda j, p: (0, j)) for _, _, count in outs]
    out_shape = [jax.ShapeDtypeStruct((count, parts * width), bf16) for _, _, count in outs]
    if norm is not None:
        in_specs += [tile_spec(k) for k in range(blocks)]
        in_specs += [rows_spec(k, norm[1].shape[1]) for k in range(blocks)] * 2
        operands += [norm[0]] * blocks + [norm[1]] * blocks + [norm[2]] * blocks
        out_specs.append(pl.BlockSpec((8, tile), lambda j, p: (0, j)))
        out_shape.append(jax.ShapeDtypeStruct((8, width), f32))
    place = jnp.stack(
        [jnp.int32(REL.index(key)) if relative else block_index(*key) for key in keys]
    ).astype(jnp.int32)
    got = pl.pallas_call(
        kernel,
        grid_spec=pltpu.PrefetchScalarGridSpec(
            num_scalar_prefetch=1,
            grid=(parts * steps,),
            in_specs=in_specs,
            out_specs=out_specs,
        ),
        out_shape=out_shape,
        compiler_params=pltpu.CompilerParams(vmem_limit_bytes=28 * 2**20),
        cost_estimate=cost(1 + blocks),
    )(place, *operands)
    found = {}
    for out, (k, inside, count) in zip(got, outs):
        if keys[k] == (2, 1):
            found.setdefault((2, 1), []).append(out)
        else:
            found[keys[k]] = out
    if norm is not None:
        return found, got[-1]
    return found


SCATTER = [
    (n, (n % (NZ * NC)) * NYH + n // (NZ * NC)) for n in range(NYH * NZ * NC)
]


def permuted(values):
    part = values.shape[1] // len(SCATTER)
    order = sorted(SCATTER, key=lambda pair: pair[1])
    return jnp.concatenate([values[:, n * part : (n + 1) * part] for n, _ in order], 1)


def relative_rows(values):
    seq_len, width = values.shape
    rows = seq_len // len(REL)

    def kernel(place_ref, in_ref, out_ref):
        out_ref[...] = permuted(in_ref[...])

    return pl.pallas_call(
        kernel,
        grid_spec=pltpu.PrefetchScalarGridSpec(
            num_scalar_prefetch=1,
            grid=(len(REL),),
            in_specs=[pl.BlockSpec((rows, width), lambda i, p: (p[i], 0))],
            out_specs=pl.BlockSpec((rows, width), lambda i, p: (i, 0)),
        ),
        out_shape=jax.ShapeDtypeStruct((seq_len, width), values.dtype),
        compiler_params=pltpu.CompilerParams(vmem_limit_bytes=16 * 2**20),
        cost_estimate=cost(4),
    )(block_places(), values)


def mlp(second, cotangent, weight):
    seq_len, width = cotangent.shape
    rows = seq_len // len(REL)
    units = weight.shape[2] // 2
    weight = weight.reshape(width, 2 * units)
    tile = min(MLP_TILE, units // 2)
    steps = units // tile
    root, cubic = (2.0 / jnp.pi) ** 0.5, 0.044715
    pieces, starts = row_pieces(second, rows)
    count = len(pieces)

    def kernel(*refs):
        cot_ref, down_ref, up_ref, du_ref, z_ref, h_ref = refs[count:]

        @pl.when(pl.program_id(0) == 0)
        def _():
            for k, start in enumerate(starts):
                h_ref[start : start + pieces[k].shape[0], :] = refs[k][...]

        u = jnp.dot(h_ref[...], up_ref[...], preferred_element_type=f32)
        dz = jnp.dot(cot_ref[...], down_ref[...], preferred_element_type=f32)
        square = u * u
        t = jnp.tanh(root * (u + cubic * (square * u)))
        half = 0.5 * (1.0 + t)
        z_ref[...] = (u * half).astype(bf16)
        slope = half + (0.5 * root) * u * (1.0 - t * t) * (1.0 + (3.0 * cubic) * square)
        du_ref[...] = (dz * slope).astype(bf16)

    once = pl.Buffered(1)
    whole = lambda shape: pl.BlockSpec(shape, lambda j: (0,) * len(shape), pipeline_mode=once)
    return pl.pallas_call(
        kernel,
        grid=(steps,),
        in_specs=[whole(piece.shape) for piece in pieces]
        + [
            whole(cotangent.shape),
            pl.BlockSpec((width, tile), lambda j: (0, j)),
            pl.BlockSpec((width, tile), lambda j: (0, steps + j)),
        ],
        out_specs=[
            pl.BlockSpec((seq_len, tile), lambda j: (0, j)),
            pl.BlockSpec((seq_len, tile), lambda j: (0, j)),
            whole((seq_len, width)),
        ],
        out_shape=[
            jax.ShapeDtypeStruct((seq_len, units), bf16),
            jax.ShapeDtypeStruct((seq_len, units), bf16),
            jax.ShapeDtypeStruct((seq_len, width), bf16),
        ],
        compiler_params=pltpu.CompilerParams(vmem_limit_bytes=MLP_VMEM * 2**20),
        cost_estimate=cost(16),
    )(*pieces, cotangent, weight, weight)


def mlp_gradients(second, grad_hidden, cotangent, active):
    seq_len, width = second.shape
    cols = active.shape[1]
    tile = min(512, width // 2)

    def kernel(h_ref, du_ref, cot_ref, z_ref, out_ref):
        over = (((0,), (0,)), ((), ()))
        out_ref[:, :cols] = lax.dot_general(
            h_ref[...], du_ref[...], over, preferred_element_type=f32
        ).astype(bf16)
        out_ref[:, cols:] = lax.dot_general(
            cot_ref[...], z_ref[...], over, preferred_element_type=f32
        ).astype(bf16)

    lhs = pl.BlockSpec((seq_len, tile), lambda i: (0, i))
    whole = pl.BlockSpec((seq_len, cols), lambda i: (0, 0))
    return pl.pallas_call(
        kernel,
        grid=(width // tile,),
        in_specs=[lhs, whole, lhs, whole],
        out_specs=pl.BlockSpec((tile, 2 * cols), lambda i: (i, 0)),
        out_shape=jax.ShapeDtypeStruct((width, 2 * cols), bf16),
        compiler_params=pltpu.CompilerParams(vmem_limit_bytes=28 * 2**20),
        cost_estimate=cost(11),
    )(second, grad_hidden, cotangent, active)


def late_gradients(first, grad_mixed, branch, attended, vectors):
    seq_len, width = first.shape
    rows = seq_len // len(REL)
    wide, narrow = grad_mixed.shape[1], attended.shape[1]
    slices = NZ * NC
    part = width // (slices * NYH)
    group = 2
    tile = group * NYH * part
    lanes = 128
    pieces, starts = row_pieces(branch, rows)
    count = len(pieces)

    def kernel(place_ref, *refs):
        h_ref, mixed_ref, o_ref, vec_ref = refs[:4]
        da_refs = refs[4 : 4 + NYH * count]
        out_ref, lhs_ref, rhs_ref = refs[4 + NYH * count :]

        @pl.when(pl.program_id(0) == 0)
        def _():
            for i in range(len(REL)):
                begin = pl.multiple_of(place_ref[i] * rows, rows)
                rhs_ref[i * rows : (i + 1) * rows, :] = o_ref[pl.ds(begin, rows), :]

        for k, start in enumerate(starts):
            stop = start + pieces[k].shape[0]
            for n in range(NYH):
                for g in range(group):
                    place = (g * NYH + n) * part
                    lhs_ref[start:stop, place : place + part] = da_refs[n * count + k][
                        :, g * part : (g + 1) * part
                    ]
        over = (((0,), (0,)), ((), ()))
        out_ref[:, :wide] = lax.dot_general(
            h_ref[...], mixed_ref[...], over, preferred_element_type=f32
        ).astype(bf16)
        out_ref[:, wide : wide + narrow] = lax.dot_general(
            lhs_ref[...], rhs_ref[...], over, preferred_element_type=f32
        ).astype(bf16)
        padded = jnp.concatenate([vec_ref[...], jnp.zeros((lanes - 8, tile), f32)], 0)
        out_ref[:, wide + narrow :] = padded.T.astype(bf16)

    whole = lambda shape: pl.BlockSpec(shape, lambda i, p: (0,) * len(shape))
    steps = slices // group
    near = [pl.BlockSpec((v.shape[0], group * part), lambda i, p: (0, i)) for v in pieces]
    far = [pl.BlockSpec((v.shape[0], group * part), lambda i, p: (0, steps + i)) for v in pieces]
    return pl.pallas_call(
        kernel,
        grid_spec=pltpu.PrefetchScalarGridSpec(
            num_scalar_prefetch=1,
            grid=(steps,),
            in_specs=[
                pl.BlockSpec((seq_len, tile), lambda i, p: (0, i)),
                whole(grad_mixed.shape),
                whole(attended.shape),
                pl.BlockSpec((8, tile), lambda i, p: (0, i)),
            ]
            + near
            + far,
            out_specs=pl.BlockSpec((tile, wide + narrow + lanes), lambda i, p: (i, 0)),
            scratch_shapes=[
                pltpu.VMEM((seq_len, tile), bf16),
                pltpu.VMEM((seq_len, narrow), bf16),
            ],
        ),
        out_shape=jax.ShapeDtypeStruct((width, wide + narrow + lanes), bf16),
        compiler_params=pltpu.CompilerParams(vmem_limit_bytes=24 * 2**20),
        cost_estimate=cost(11),
    )(block_places(), first, grad_mixed, attended, vectors, *pieces, *pieces)


def scatter_order(values):
    shape = values.shape
    values = values.reshape(shape[:-1] + (NYH, NZ * NC, -1))
    return jnp.swapaxes(values, -3, -2).reshape(shape)


def pair_yh(own):
    other = lax.ppermute(own, "yh", [(0, 1), (1, 0)])
    first = lax.axis_index("yh") == 0
    return jnp.stack([jnp.where(first, own, other), jnp.where(first, other, own)], 0)


def gather_zc(pair):
    return lax.all_gather(pair, ("z", "c"), axis=0, tiled=True)


def scatter_dp(values):
    values = lax.psum_scatter(values, ("z", "c"), scatter_dimension=0, tiled=True)
    yh = lax.axis_index("yh")
    rows = values.shape[0] // NYH
    home = lax.dynamic_slice_in_dim(values, yh * rows, rows, 0)
    away = lax.dynamic_slice_in_dim(values, (1 - yh) * rows, rows, 0)
    return up(home) + up(lax.ppermute(away, "yh", [(0, 1), (1, 0)]))


def on_own_rows(body, terms, row_arrays, own_arrays, gains, outs):
    rows = terms[0].shape[0]
    ins = terms + row_arrays + own_arrays + gains

    def kernel(place_ref, *refs):
        values = [ref[...] for ref in refs[: len(ins)]]
        total = up(values[0])
        for value in values[1 : len(terms)]:
            total = total + up(value)
        results = body(total, *values[len(terms) :])
        for ref, result in zip(refs[len(ins) :], results):
            ref[...] = result.astype(ref.dtype)

    whole = lambda shape: pl.BlockSpec(shape, lambda i, p: (0, 0))
    return pl.pallas_call(
        kernel,
        grid_spec=pltpu.PrefetchScalarGridSpec(
            num_scalar_prefetch=1,
            grid=(1,),
            in_specs=[whole(v.shape) for v in terms]
            + [pl.BlockSpec((rows, v.shape[1]), lambda i, p: (p[0], 0)) for v in row_arrays]
            + [whole(v.shape) for v in own_arrays + gains],
            out_specs=[whole(shape) for shape, _ in outs],
        ),
        out_shape=[jax.ShapeDtypeStruct(shape, dtype) for shape, dtype in outs],
        compiler_params=pltpu.CompilerParams(vmem_limit_bytes=32 * 2**20),
        cost_estimate=SMALL,
    )(block_index(0, 0).astype(jnp.int32).reshape(1), *ins)


def norm_and_qkv(tokens, mine, other, cols):
    seq_len, width = tokens.shape
    slices, packed_rows, all_cols = mine.shape
    shard = packed_rows - 16
    tile = min(256, seq_len // 4)

    def kernel(
        place_ref, x_ref, mine_ref, other_ref, h_ref, qkv_ref, w_ref, vec_ref, mean_ref, inverse_ref
    ):
        core = place_ref[0]

        @pl.when(pl.program_id(0) == 0)
        def _():
            for ref, parity in ((mine_ref, core), (other_ref, 1 - core)):
                for s in range(slices):
                    begin = pl.multiple_of((NC * s + parity) * shard, shard)
                    w_ref[pl.ds(begin, shard), :] = ref[s, :shard, :]
                    row = ref[s, shard:, :].astype(f32)
                    for k in range(4):
                        vec_ref[k : k + 1, pl.ds(begin, shard)] = row[
                            0:1, k * shard : (k + 1) * shard
                        ]

        x = x_ref[...].astype(f32)
        mean = jnp.mean(x, axis=-1, keepdims=True)
        center = x - mean
        inverse = lax.rsqrt(jnp.mean(center * center, axis=-1, keepdims=True) + eps)
        mean_ref[...] = jnp.broadcast_to(mean, mean_ref.shape)
        inverse_ref[...] = jnp.broadcast_to(inverse, inverse_ref.shape)
        h = (center * inverse * vec_ref[0:1, :] + vec_ref[1:2, :]).astype(bf16)
        for n in range(NYH * NZ * NC):
            place = (n % (NZ * NC)) * NYH + n // (NZ * NC)
            h_ref[:, place * shard : (place + 1) * shard] = h[:, n * shard : (n + 1) * shard]
        qkv_ref[...] = jnp.dot(h, w_ref[:, :cols], preferred_element_type=f32).astype(bf16)

    whole = lambda shape: pl.BlockSpec(shape, lambda i, p: (0,) * len(shape))
    place = lax.axis_index("c").astype(jnp.int32).reshape(1)
    return pl.pallas_call(
        kernel,
        grid_spec=pltpu.PrefetchScalarGridSpec(
            num_scalar_prefetch=1,
            grid=(seq_len // tile,),
            in_specs=[
                pl.BlockSpec((tile, width), lambda i, p: (i, 0)),
                whole(mine.shape),
                whole(other.shape),
            ],
            out_specs=[
                pl.BlockSpec((tile, width), lambda i, p: (i, 0)),
                pl.BlockSpec((tile, cols), lambda i, p: (i, 0)),
                whole((width, all_cols)),
                whole((8, width)),
                pl.BlockSpec((tile, 128), lambda i, p: (i, 0)),
                pl.BlockSpec((tile, 128), lambda i, p: (i, 0)),
            ],
        ),
        out_shape=[
            jax.ShapeDtypeStruct((seq_len, width), bf16),
            jax.ShapeDtypeStruct((seq_len, cols), bf16),
            jax.ShapeDtypeStruct((width, all_cols), bf16),
            jax.ShapeDtypeStruct((8, width), f32),
            jax.ShapeDtypeStruct((seq_len, 128), f32),
            jax.ShapeDtypeStruct((seq_len, 128), f32),
        ],
        compiler_params=pltpu.CompilerParams(vmem_limit_bytes=36 * 2**20),
        cost_estimate=cost(9),
    )(place, tokens, mine, other)


def scores_of(query, keys, begin, ends_ref, scale):
    rows, seen = query.shape[0], keys.shape[0]
    scores = (
        lax.dot_general(query, keys, (((1,), (1,)), ((), ())), preferred_element_type=f32) * scale
    )
    place = begin + lax.broadcasted_iota(jnp.int32, (rows, 1), 0)
    first = jnp.zeros((rows, 1), jnp.int32)
    for k in range(4):
        first = jnp.where(place >= ends_ref[k], ends_ref[k], first)
    column = lax.broadcasted_iota(jnp.int32, (rows, seen), 1)
    return jnp.where((column >= first) & (column <= place), scores, f32(-1e30))


def attend(qkv, ends, scale):
    seq_len, cols = qkv.shape
    heads = cols // (3 * HEAD_SIZE)
    tile = min(256, seq_len // 4)

    def kernel(ends_ref, q_ref, k_ref, v_ref, o_ref, lse_ref):
        for begin in range(0, seq_len, tile):
            seen = begin + tile
            scores = scores_of(q_ref[begin:seen, :], k_ref[:seen, :], begin, ends_ref, scale)
            largest = jnp.max(scores, axis=-1, keepdims=True)
            expo = jnp.exp(scores - largest)
            totals = jnp.sum(expo, axis=-1, keepdims=True)
            probs = (expo / totals).astype(bf16)
            o_ref[begin:seen, :] = jnp.dot(
                probs, v_ref[:seen, :], preferred_element_type=f32
            ).astype(bf16)
            lse_ref[begin:seen, :] = jnp.broadcast_to(
                largest + jnp.log(totals), (tile, HEAD_SIZE)
            )

    def spec(kind):
        return pl.BlockSpec((seq_len, HEAD_SIZE), lambda h, e: (0, kind * heads + h))

    return pl.pallas_call(
        kernel,
        grid_spec=pltpu.PrefetchScalarGridSpec(
            num_scalar_prefetch=1,
            grid=(heads,),
            in_specs=[spec(0), spec(1), spec(2)],
            out_specs=[spec(0), spec(0)],
        ),
        out_shape=[
            jax.ShapeDtypeStruct((seq_len, heads * HEAD_SIZE), bf16),
            jax.ShapeDtypeStruct((seq_len, heads * HEAD_SIZE), f32),
        ],
        compiler_params=pltpu.CompilerParams(vmem_limit_bytes=24 * 2**20),
        cost_estimate=cost(6),
    )(ends, qkv, qkv, qkv)


def attend_back(qkv, lse, branch, weight, ends, scale):
    seq_len, cols = qkv.shape
    heads = cols // (3 * HEAD_SIZE)
    own = heads * HEAD_SIZE
    width = weight.shape[0]
    rows = seq_len // len(REL)
    tile = min(256, seq_len // 4)
    pieces, starts = row_pieces(branch, rows)
    count = len(pieces)

    def kernel(ends_ref, place_ref, *refs):
        q_ref, k_ref, v_ref, lse_ref, w_ref = refs[:5]
        out_ref, dk_ref, dv_ref, da_ref, go_ref = refs[5 + count :]
        h = pl.program_id(0)

        @pl.when(h == 0)
        def _():
            for k, start in enumerate(starts):
                i, inside = start // rows, start % rows
                begin = pl.multiple_of(place_ref[i] * rows + inside, rows // 2)
                da_ref[pl.ds(begin, pieces[k].shape[0]), :] = refs[5 + k][...]
            grad = jnp.dot(da_ref[...], w_ref[...], preferred_element_type=f32).astype(bf16)
            for n in range(heads):
                go_ref[n] = grad[:, n * HEAD_SIZE : (n + 1) * HEAD_SIZE]

        def columns(kind):
            return pl.ds(pl.multiple_of((kind * heads + h) * HEAD_SIZE, HEAD_SIZE), HEAD_SIZE)

        dk_ref[...] = jnp.zeros_like(dk_ref)
        dv_ref[...] = jnp.zeros_like(dv_ref)
        for begin in range(0, seq_len, tile):
            seen = begin + tile
            query = q_ref[begin:seen, :]
            scores = scores_of(query, k_ref[:seen, :], begin, ends_ref, scale)
            probs = jnp.exp(scores - lse_ref[begin:seen, 0:1])
            grad = go_ref[h, begin:seen, :]
            grad_probs = lax.dot_general(
                grad, v_ref[:seen, :], (((1,), (1,)), ((), ())), preferred_element_type=f32
            )
            inner = jnp.sum(probs * grad_probs, axis=-1, keepdims=True)
            grad_scores = (probs * (grad_probs - inner)).astype(bf16)
            out_ref[begin:seen, columns(0)] = (
                jnp.dot(grad_scores, k_ref[:seen, :], preferred_element_type=f32) * scale
            ).astype(bf16)
            over_rows = (((0,), (0,)), ((), ()))
            dk_ref[:seen, :] += lax.dot_general(
                grad_scores, query, over_rows, preferred_element_type=f32
            )
            dv_ref[:seen, :] += lax.dot_general(
                probs.astype(bf16), grad, over_rows, preferred_element_type=f32
            )
        out_ref[:, columns(1)] = (dk_ref[...] * scale).astype(bf16)
        out_ref[:, columns(2)] = dv_ref[...].astype(bf16)

    def spec(kind):
        return pl.BlockSpec((seq_len, HEAD_SIZE), lambda h, e, p: (0, kind * heads + h))

    whole = lambda shape: pl.BlockSpec(shape, lambda h, e, p: (0,) * len(shape))
    return pl.pallas_call(
        kernel,
        grid_spec=pltpu.PrefetchScalarGridSpec(
            num_scalar_prefetch=2,
            grid=(heads,),
            in_specs=[
                spec(0),
                spec(1),
                spec(2),
                spec(0),
                pl.BlockSpec((width, own), lambda h, e, p: (0, cols // own)),
            ]
            + [whole(piece.shape) for piece in pieces],
            out_specs=whole((seq_len, cols)),
            scratch_shapes=[
                pltpu.VMEM((seq_len, HEAD_SIZE), f32),
                pltpu.VMEM((seq_len, HEAD_SIZE), f32),
                pltpu.VMEM((seq_len, width), bf16),
                pltpu.VMEM((heads, seq_len, HEAD_SIZE), bf16),
            ],
        ),
        out_shape=jax.ShapeDtypeStruct((seq_len, cols), bf16),
        compiler_params=pltpu.CompilerParams(vmem_limit_bytes=36 * 2**20),
        cost_estimate=cost(12),
    )(ends, block_places(), qkv, qkv, qkv, lse, weight, *pieces)


def local(
    tokens,
    doc_lengths,
    gain_one,
    bias_one,
    w_qkv,
    w_out,
    gain_two,
    bias_two,
    w_up,
    w_down,
    cotangent,
):
    seq_len, width = tokens.shape
    shard = w_qkv.shape[0]
    local_width = w_qkv.shape[2]
    local_heads = local_width // HEAD_SIZE
    rows = seq_len // (NX * NYL)
    x, y = lax.axis_index("x"), lax.axis_index("yl")
    scale = HEAD_SIZE**-0.5

    wide = 3 * local_width
    small = jnp.stack([gain_one, bias_one, gain_two, bias_two], 0).astype(bf16)
    small = jnp.pad(small.reshape(1, -1), ((0, 15), (0, wide + local_width - 4 * shard)))
    packed = jnp.concatenate([w_qkv.reshape(shard, wide).astype(bf16), w_out.astype(bf16)], 1)
    first_mine = gather_yz(jnp.concatenate([packed, small], 0))
    first_other = lax.ppermute(first_mine, "c", [(0, 1), (1, 0)])
    cot_order = relative_rows(cotangent)
    ends = jnp.cumsum(doc_lengths[0])

    first, mixed, weight, vectors, mean_one, inverse_one = norm_and_qkv(
        tokens, first_mine, first_other, wide
    )
    mlp_weight = jnp.concatenate([w_down.astype(bf16), w_up.astype(bf16)], 1)
    mlp_weight = pair_yh(after(mlp_weight, first_other))
    gain_a, gain_b, bias_b = vectors[0], vectors[2], vectors[3]
    attended, lse = attend(mixed, ends, scale)
    terms = terms_by_block(STEP_ONE, [attended], weight, first=3)
    sum_one = scatter_one(terms)
    later = terms_by_block(LATER_STEPS, [after(attended, *terms[2, 1])], weight, first=3)
    mlp_weight = gather_zc(after(mlp_weight, attended))
    own_f32, own_bf16 = ((rows, width), f32), ((rows, width), bf16)
    gain_a, gain_b, bias_b = (v.reshape(1, width) for v in (gain_a, gain_b, bias_b))

    def second_norm(branch, x, gain, bias):
        middle = up(x) + branch
        normed, _ = normalize(middle)
        return middle, permuted((normed * gain + bias).astype(bf16))

    own_middle, second = on_own_rows(
        second_norm,
        scatter_three(later, scatter_two(later, sum_one)),
        [tokens],
        [],
        [gain_b, bias_b],
        [own_f32, own_bf16],
    )

    second_one = gather_one(second)
    second_two = gather_two(second_one)
    grad_hidden, active, second = mlp(
        gather_three(second, second_one, second_two), cot_order, mlp_weight
    )
    hidden = [active, grad_hidden]
    terms = terms_by_block(STEP_ONE, hidden, mlp_weight, relative=True)
    sum_one = scatter_one(terms)
    later = terms_by_block(
        LATER_STEPS, after(hidden, *terms[2, 1]), mlp_weight, relative=True
    )
    sum_two = scatter_two(later, sum_one)
    both = scatter_three(later, sum_two)
    mlp_terms = mlp_gradients(after(second, sum_two[2]), grad_hidden, cot_order, active)
    both = after(both, mlp_terms)
    mlp_grads = scatter_dp(mlp_terms)
    grad_up, grad_down = mlp_grads[:, : w_up.shape[1]], mlp_grads[:, w_up.shape[1] :]

    def second_norm_back(both, cot, middle, gain):
        grad = both[:, width:]
        normed, inverse = normalize(middle)
        vector = jnp.concatenate(
            [
                jnp.sum(grad * normed, axis=0, keepdims=True),
                jnp.sum(grad, axis=0, keepdims=True),
                jnp.zeros((6, width), f32),
            ],
            0,
        )
        back = up(cot) + norm_back(grad, normed, inverse, gain)
        return middle + both[:, :width], back, back, vector

    output_own, grad_middle, own_branch, vec_two = on_own_rows(
        second_norm_back,
        both,
        [cotangent],
        [own_middle],
        [gain_b],
        [own_bf16, own_f32, own_bf16, ((8, width), f32)],
    )
    branch_one = gather_one(own_branch)
    branch_two = gather_two(branch_one)
    branch = gather_three(own_branch, branch_one, branch_two)
    output_one = gather_one(after(output_own, branch_two[0]))
    grad_mixed = attend_back(mixed, lse, branch, weight, ends, scale)
    norm = (tokens, mean_one, inverse_one)
    terms, vec_a = terms_by_block(STEP_ONE, [grad_mixed], weight, norm=norm)
    sum_one = scatter_one(terms)
    later, vec_b = terms_by_block(
        LATER_STEPS, [after(grad_mixed, *terms[2, 1])], weight, norm=norm
    )
    sum_two = scatter_two(later, sum_one)
    vec_one = vec_a + vec_b
    late_vectors = scatter_order(
        jnp.concatenate([vec_one[:2], vec_two[:2], jnp.zeros((4, width), f32)], 0)
    )
    grad_first = scatter_three(later, sum_two)
    late = late_gradients(after(first, *sum_one), grad_mixed, branch, attended, late_vectors)
    late = scatter_dp(late)

    def first_norm_back(grad, x, middle, gain):
        normed, inverse = normalize(up(x))
        return [middle + norm_back(grad, normed, inverse, gain)]

    (grad_tokens,) = on_own_rows(
        first_norm_back, grad_first, [tokens], [grad_middle], [gain_a], [own_bf16]
    )
    output = gather_three(output_own, output_one, gather_two(output_one))
    output = assemble(output, width, bf16, 0)
    grad_one = gather_one(grad_tokens)
    input_grad = gather_three(grad_tokens, grad_one, gather_two(grad_one))
    sums = sum_mp(late[:, wide + local_width : wide + local_width + 4].T)
    input_grad, sums = lax.optimization_barrier((input_grad, sums))
    input_grad = assemble(input_grad, width, f32, 0)
    return (
        output,
        input_grad,
        sums[0],
        sums[1],
        late[:, :wide].reshape(shard, 3, local_width),
        late[:, wide : wide + local_width],
        sums[2],
        sums[3],
        grad_up,
        grad_down,
    )


def solution(mesh):
    fine = Mesh(mesh.devices.reshape(NYH, NZ, NC, NX, NYL), ("yh", "z", "c", "x", "yl"))
    return jax.shard_map(
        local,
        mesh=fine,
        in_specs=(
            P(DP, None),
            P(DP, None),
            P(DP),
            P(DP),
            P(DP, None, MP),
            P(DP, MP),
            P(DP),
            P(DP),
            P(DP, MP),
            P(DP, MP),
            P(DP, None),
        ),
        out_specs=(
            P(DP, None),
            P(DP, None),
            P(DP),
            P(DP),
            P(DP, None, MP),
            P(DP, MP),
            P(DP),
            P(DP),
            P(DP, MP),
            P(DP, MP),
        ),
        check_vma=False,
    )
```
